128 devices in a mesh: row: 4 (over z), col: 32 (over y, x, core).
Axes of the slice: x: 4, y: 4, z: 4, core: 2. Of those that a mesh axis runs over, the one named last changes fastest.
Arguments:
- tokens: bfloat16 [128, 512, 512], P('row', 'col'), may hold values from -6 to 6
- tile_mask: int32 [8, 32], P('row', 'col'), may hold values 0 or 1
- norm_gain: float32 [512], replicated, may hold values from 0.5 to 1.5
- w_in: bfloat16 [512, 2048], P(None, ('row', 'col')), may hold values from -0.25 to 0.25
- conv_weight: float32 [9, 1024], replicated, may hold values from -2 to 2
- conv_bias: float32 [1024], replicated, may hold values from -3 to 3
- w_proj: bfloat16 [1024, 256], P(('row', 'col')), may hold values from -0.1875 to 0.1875
- dt_bias: float32 [4, 32], replicated, may hold values from 0.25 to 1.25
- decay_rate: float32 [4, 32], replicated, may hold values from 0.006 to 0.12, as said below
- skip_gain: float32 [1024], replicated, may hold values from 0.5 to 1.5
- out_gain: float32 [1024], replicated, may hold values from 0.5 to 1.5
- w_out: bfloat16 [1024, 512], P(('row', 'col')), may hold values from -0.1875 to 0.1875
Outputs:
- result: bfloat16 [128, 512, 512], P('row', 'col')
The draws below stay inside these ranges and needn't reach their ends.
Inputs may be any that keep to these rules, and one draw needn't show every extreme that they name: `decay_rate`: decay rates of each direction and head.
All inputs are finite; a program needn't handle non-finite values. No bound on the sum of `tile_mask` on one device may be relied on, other than what follows from the above.
Results may differ from the reference program's by a relative error of at most 0.01.
Values may be sent and summed in bfloat16 or wider, within the bound.
No kernel may reach another device: no remote copies, remote signals or barrier semaphores. Data moves between devices by JAX's collectives and lax.ppermute only.
A program may use at most 448 MiB of HBM per device.

```python
import math
import jax
import jax.numpy as jnp
from jax import lax

CHANNELS = 512
EXPAND = 1024
STATE = 16
HEADS = 32
DIRS = 4
BLOCK = 16
TILE = 16
PROJ = 256
ROWS = 128
COLS = 512


def draw_decay_rate(key, part):
    slow_key = jax.random.fold_in(key, 12)
    rates = jnp.exp(jax.random.uniform(slow_key, (DIRS, HEADS), jnp.float32, math.log(0.006), math.log(0.12)))
    return rates.astype(jnp.float32)


def set_ends(entries, key, low, top_value):
    place = [jax.random.randint(jax.random.fold_in(key, axis), (), 0, length) for axis, length in enumerate(entries.shape)]
    widest = entries.shape.index(max(entries.shape))
    beside = place[:widest] + [(place[widest] + 1) % entries.shape[widest]] + place[widest + 1:]
    return entries.at[tuple(place)].set(low).at[tuple(beside)].set(top_value)


def block_scale(own_key, extent, split, low, top_value):
    def one(axis_at, shards_of):
        draws = jax.random.uniform(jax.random.fold_in(jax.random.fold_in(own_key, 6), axis_at), (shards_of,), jnp.float32, low / len(split), top_value / len(split))
        return jnp.repeat(jnp.exp(draws), extent[axis_at] // shards_of).reshape((-1,) + (1,) * (len(extent) - axis_at - 1))

    level = one(*split[0])
    for cut in split[1:]:
        level = level * one(*cut)
    return level


def normal_values(own_key, shape, deviation, most, pieces=(), dtype=jnp.bfloat16):
    factor_of = block_scale(own_key, shape, pieces, -0.22, 0.18) if pieces else 1.0
    entries = jax.random.normal(own_key, shape, jnp.float32) * deviation * factor_of
    return jnp.minimum(jnp.maximum(entries, -most), most).astype(dtype)


def setup_inputs(seed: int = 0) -> dict:
    keys = jax.random.split(jax.random.key(seed), 13)
    return {
        "tokens": normal_values(keys[0], (ROWS, COLS, CHANNELS), 1.0, 6.0, ((0, 4), (1, 32))),
        "tile_mask": set_ends((jax.random.randint(keys[1], (ROWS // TILE, COLS // TILE), 0, 5) < 1).astype(jnp.int32), jax.random.fold_in(keys[1], 1), 0, 1),
        "norm_gain": jnp.clip(1.0 + 0.1 * jax.random.normal(keys[2], (CHANNELS,), jnp.float32), 0.5, 1.5),
        "w_in": normal_values(keys[3], (CHANNELS, 2 * EXPAND), CHANNELS ** -0.5, 0.25, ((1, 128),)),
        "conv_weight": normal_values(keys[4], (9, EXPAND), 9 ** -0.5, 2.0, (), jnp.float32),
        "conv_bias": normal_values(keys[5], (EXPAND,), 0.5, 3.0, (), jnp.float32),
        "w_proj": normal_values(keys[6], (EXPAND, PROJ), EXPAND ** -0.5, 0.1875, ((0, 128),)),
        "dt_bias": jnp.clip(jax.random.uniform(keys[7], (DIRS, HEADS), jnp.float32, 0.25, 1.25), 0.25, 1.25),
        "decay_rate": draw_decay_rate(jax.random.fold_in(keys[12], 71), 0),
        "skip_gain": jnp.clip(jax.random.uniform(keys[9], (EXPAND,), jnp.float32, 0.5, 1.5), 0.5, 1.5),
        "out_gain": jnp.clip(1.0 + 0.1 * jax.random.normal(keys[10], (EXPAND,), jnp.float32), 0.5, 1.5),
        "w_out": normal_values(keys[11], (EXPAND, CHANNELS), EXPAND ** -0.5, 0.1875, ((0, 128),)),
    }


highest = lax.Precision.HIGHEST

def layer_norm(values, factor):
    average = lax.optimization_barrier(jnp.mean(values, axis=-1, keepdims=True))
    centered = values - average
    spread = lax.optimization_barrier(jnp.mean(centered * centered, axis=-1, keepdims=True))
    return centered * lax.rsqrt(spread + 1e-05) * factor

def block_terms(inputs, step_sizes, write_coef, read_coef, decays, block_len):
    line_count, length, expand = inputs.shape
    heads = step_sizes.shape[-1]
    blocks = length // block_len
    states = write_coef.shape[-1]
    values = inputs.reshape(line_count, blocks, block_len, heads, expand // heads)
    step_blk = step_sizes.reshape(line_count, blocks, block_len, heads)
    write_blk = write_coef.reshape(line_count, blocks, block_len, states)
    read_blk = read_coef.reshape(line_count, blocks, block_len, states)
    cumulative = jnp.cumsum(-step_blk * decays, axis=2)
    affinity = jnp.einsum('lbtn,lbsn->lbts', read_blk, write_blk, precision=highest)
    target_idx = lax.broadcasted_iota(jnp.int32, (block_len, block_len), 0)
    source_idx = lax.broadcasted_iota(jnp.int32, (block_len, block_len), 1)
    causal = (source_idx <= target_idx)[None, None, None]
    cum_heads = jnp.moveaxis(cumulative, 3, 2)
    difference = cum_heads[:, :, :, :, None] - cum_heads[:, :, :, None, :]
    step_heads = jnp.moveaxis(step_blk, 3, 2)
    mixing = jnp.where(causal, affinity[:, :, None] * jnp.exp(jnp.where(causal, difference, 0.0)) * step_heads[:, :, :, None, :], 0.0).astype(jnp.bfloat16)
    local_out = jnp.einsum('lbhts,lbshp->lbthp', mixing, values, preferred_element_type=jnp.float32)
    tail_weight = jnp.exp(cumulative[:, :, -1:, :] - cumulative) * step_blk
    weighted = values.astype(jnp.float32) * tail_weight[..., None]
    zstate = jnp.einsum('lbshp,lbsn->lbhpn', weighted, write_blk, precision=highest)
    bdecay = jnp.exp(cumulative[:, :, -1, :])
    return (local_out, cumulative, read_blk, zstate, bdecay)

def block_prefix(zstate, bdecay):
    line_count, blocks, heads, head_dim, states = zstate.shape

    def advance(carried, current):
        running, product = carried
        block_state, block_decay = current
        return ((block_decay[:, :, None, None] * running + block_state, block_decay * product), (running, product))
    initial = (jnp.zeros((line_count, heads, head_dim, states), jnp.float32), jnp.ones((line_count, heads), jnp.float32))
    closing, entering = lax.scan(advance, initial, (jnp.moveaxis(zstate, 1, 0), jnp.moveaxis(bdecay, 1, 0)))
    return (jnp.moveaxis(entering[0], 0, 1), jnp.moveaxis(entering[1], 0, 1), closing[0], closing[1])

def readout(local_out, cumulative, read_blk, entering):
    line_count, blocks, block_len, heads, head_dim = local_out.shape
    carried = jnp.einsum('lbtn,lbhpn->lbthp', read_blk, entering, precision=highest)
    combined = local_out + jnp.exp(cumulative)[..., None] * carried
    return combined.reshape(line_count, blocks * block_len, heads * head_dim)

def direction_line(inputs, step_sizes, write_coef, read_coef, decays):
    local_out, cumulative, read_blk, zstate, bdecay = block_terms(inputs, step_sizes, write_coef, read_coef, decays, BLOCK)
    entering, before, closing_state, closing_decay = block_prefix(zstate, bdecay)
    return readout(local_out, cumulative, read_blk, entering)

def sweep(inputs, step_sizes, write_coef, read_coef, decays):
    line_count = inputs.shape[0]
    batch_lines = 8

    def one_group(group):
        return direction_line(group[0], group[1], group[2], group[3], decays)
    grouped = tuple((array.reshape((line_count // batch_lines, batch_lines) + array.shape[1:]) for array in (inputs, step_sizes, write_coef, read_coef)))
    swept = lax.map(one_group, grouped)
    return swept.reshape((line_count,) + swept.shape[2:])

def reference(tokens, tile_mask, norm_gain, w_in, conv_weight, conv_bias, w_proj, dt_bias, decay_rate, skip_gain, out_gain, w_out):
    height, breadth, channels = tokens.shape
    expand = w_out.shape[0]
    normed = layer_norm(tokens.astype(jnp.float32), norm_gain).astype(jnp.bfloat16)
    flat = normed.reshape(height * breadth, channels)
    branch = jnp.dot(flat, w_in[:, :expand], preferred_element_type=jnp.float32).astype(jnp.bfloat16).reshape(height, breadth, expand)
    gating = jnp.dot(flat, w_in[:, expand:], preferred_element_type=jnp.float32).astype(jnp.bfloat16).reshape(height, breadth, expand)
    padded = jnp.pad(branch, ((1, 1), (1, 1), (0, 0)))
    convolved = conv_bias * jnp.ones((height, breadth, expand), jnp.float32)
    for row_tap in range(3):
        for col_tap in range(3):
            convolved = convolved + padded[row_tap:row_tap + height, col_tap:col_tap + breadth].astype(jnp.float32) * conv_weight[3 * row_tap + col_tap]
    activated = jax.nn.silu(convolved).astype(jnp.bfloat16)
    coefs_all = jnp.dot(activated.reshape(height * breadth, expand), w_proj, preferred_element_type=jnp.float32).reshape(height, breadth, -1)
    kept = jnp.broadcast_to(tile_mask[:, None, :, None], (height // TILE, TILE, breadth // TILE, TILE)).reshape(height, breadth).astype(jnp.float32)
    group_len = HEADS + 2 * STATE
    summed = skip_gain * activated.astype(jnp.float32)
    for direction in range(4):
        coef_block = coefs_all[..., direction * group_len:(direction + 1) * group_len]
        step_sizes = kept[..., None] * jax.nn.softplus(coef_block[..., :HEADS] + dt_bias[direction])
        write_coef = coef_block[..., HEADS:HEADS + STATE]
        read_coef = coef_block[..., HEADS + STATE:]
        arrays = (activated, step_sizes, write_coef, read_coef)
        if direction >= 2:
            arrays = tuple((jnp.swapaxes(array, 0, 1) for array in arrays))
        if direction % 2 == 1:
            arrays = tuple((array[:, ::-1] for array in arrays))
        swept = sweep(arrays[0], arrays[1], arrays[2], arrays[3], decay_rate[direction])
        if direction % 2 == 1:
            swept = swept[:, ::-1]
        if direction >= 2:
            swept = jnp.swapaxes(swept, 0, 1)
        summed = summed + swept
    mixed = (layer_norm(summed, out_gain) * jax.nn.silu(gating.astype(jnp.float32))).astype(jnp.bfloat16)
    projected = jnp.dot(mixed.reshape(height * breadth, expand), w_out, preferred_element_type=jnp.float32).reshape(height, breadth, channels)
    return (tokens.astype(jnp.float32) + projected).astype(jnp.bfloat16)
```

```python
import functools

import jax
import jax.numpy as jnp
from jax import lax
from jax.experimental import pallas as pl
from jax.experimental.pallas import tpu as pltpu
from jax.sharding import PartitionSpec as P

STATE = 16
HEADS = 32
TILE = 16
CHUNK = 128
LANES = 128
STRIDE = 24
LOG2E = 1.4426950408889634

f32 = jnp.float32
bf16 = jnp.bfloat16


def dot(a, b, contract=((1,), (0,))):
    return lax.dot_general(a, b, (contract, ((), ())), preferred_element_type=f32)


def shifted(x, axis, step):
    count = lax.axis_size(axis)
    pairs = [(i, i + step) for i in range(count) if 0 <= i + step < count]
    return lax.ppermute(x, axis, pairs)


def normalized(x, gain):
    average = jnp.mean(x, axis=-1, keepdims=True)
    centered = x - average
    spread = jnp.mean(centered * centered, axis=-1, keepdims=True)
    return centered * lax.rsqrt(spread + 1e-05) * gain


def filter_kernel(
    x_ref, gain_ref, w_ref, taps_ref, bias_ref, act_ref, turned_ref, normed, branch, order
):
    padded = x_ref.shape[0]
    tokens, width = act_ref.shape
    height = padded // STRIDE - 2
    breadth = tokens // height

    @pl.when(pl.program_id(0) == 0)
    def _():
        step = 64
        for at in range(0, padded, step):
            x = x_ref[at : at + step, :].astype(f32)
            normed[at : at + step, :] = normalized(x, gain_ref[...]).astype(bf16)
        to = lax.broadcasted_iota(jnp.int32, (tokens, tokens), 0)
        source = lax.broadcasted_iota(jnp.int32, (tokens, tokens), 1)
        w, h = to // height, to % height
        order[...] = (source == h * breadth + w).astype(f32).astype(bf16)

    product = dot(normed[...], w_ref[...], ((1,), (1,)))
    branch[...] = product.astype(bf16).astype(f32)
    rows = 4
    span = rows * STRIDE + 8
    for lane in range(0, width, LANES):
        lanes = slice(lane, lane + LANES)
        taps = [taps_ref[k : k + 1, lanes] for k in range(9)]
        for h in range(0, height, rows):
            windows = [
                branch[(h + i) * STRIDE : (h + i) * STRIDE + span, lanes] for i in range(3)
            ]
            left, middle, right = [
                windows[0] * taps[j] + windows[1] * taps[3 + j] + windows[2] * taps[6 + j]
                for j in range(3)
            ]
            convolved = (
                middle
                + pltpu.roll(left, 1, 0)
                + pltpu.roll(right, span - 1, 0)
                + bias_ref[:, lanes]
            )
            activated = convolved / (1.0 + jnp.exp(-convolved))
            kept = activated[: rows * STRIDE].reshape(rows, STRIDE, LANES)[:, 8:, :]
            act_ref[h * breadth : (h + rows) * breadth, lanes] = kept.reshape(
                rows * breadth, LANES
            ).astype(bf16)
    turned_ref[...] = dot(order[...], act_ref[...]).astype(bf16)


def filtered(x, gain, w_in, taps, bias, tokens):
    expand = bias.shape[1]
    padded, channels = x.shape
    width = 256
    return pl.pallas_call(
        filter_kernel,
        grid=(expand // width,),
        in_specs=[
            pl.BlockSpec((padded, channels), lambda c: (0, 0)),
            pl.BlockSpec((1, channels), lambda c: (0, 0)),
            pl.BlockSpec((width, channels), lambda c: (c, 0)),
            pl.BlockSpec((9, width), lambda c: (0, c)),
            pl.BlockSpec((1, width), lambda c: (0, c)),
        ],
        out_specs=[
            pl.BlockSpec((tokens, width), lambda c: (0, c)),
            pl.BlockSpec((tokens, width), lambda c: (0, c)),
        ],
        out_shape=[jax.ShapeDtypeStruct((tokens, expand), bf16)] * 2,
        scratch_shapes=[
            pltpu.VMEM((padded, channels), bf16),
            pltpu.VMEM((padded, width), f32),
            pltpu.VMEM((tokens, tokens), bf16),
        ],
        compiler_params=pltpu.CompilerParams(vmem_limit_bytes=48 * 2**20),
        name="norm_project_filter",
    )(x, gain, w_in, taps, bias)


def chunk_terms(values, w_proj, bias, rate, mask, first):
    coefs = dot(values, w_proj)
    at = lax.broadcasted_iota(jnp.int32, (CHUNK, LANES), 0)
    lane = lax.broadcasted_iota(jnp.int32, (CHUNK, LANES), 1)
    kept = jnp.sum(
        jnp.where(lane == (at + first) // TILE, mask, 0.0), axis=1, keepdims=True
    )
    v = coefs + bias
    steps = kept * (jnp.maximum(v, 0.0) + jnp.log1p(jnp.exp(-jnp.abs(v))))
    decays = steps * rate
    lower = (lane <= at).astype(f32).astype(bf16)
    high = decays.astype(bf16)
    rest = decays - high.astype(f32)
    middle = rest.astype(bf16)
    low = (rest - middle.astype(f32)).astype(bf16)
    total = dot(lower, high) + (dot(lower, middle) + dot(lower, low))
    sums = jnp.where(lane < 64, total, total - decays)
    return coefs, steps, sums, total[CHUNK - 1 :, :]


def local_weights(coefs):
    at = lax.broadcasted_iota(jnp.int32, (CHUNK, CHUNK), 0)
    source = lax.broadcasted_iota(jnp.int32, (CHUNK, CHUNK), 1)
    c = coefs.astype(bf16)
    forward = dot(c[:, 48:64], c[:, 32:48], ((1,), (1,)))
    backward = dot(c[:, 112:128], c[:, 96:112], ((1,), (1,)))
    return (
        source <= at,
        jnp.where(source <= at, forward, 0.0),
        jnp.where(source >= at, backward, 0.0),
    )


def local_tile(values, tile, weights, sums, sums_t, steps_t):
    causal, forward, backward = weights
    lane = lax.broadcasted_iota(jnp.int32, (CHUNK, LANES), 1)
    inputs = values[:, tile * LANES : (tile + 1) * LANES]
    mixing, sources = [], []
    for k in range(4):
        j = 4 * tile + k
        exponent = jnp.where(
            causal,
            sums_t[j : j + 1, :] - sums[:, j : j + 1],
            sums[:, 64 + j : 65 + j] - sums_t[64 + j : 65 + j, :],
        )
        scale = forward * steps_t[j : j + 1, :] + backward * steps_t[64 + j : 65 + j, :]
        mixing.append(jnp.exp2(exponent) * scale)
        sources.append(jnp.where(lane // 32 == k, inputs, jnp.zeros_like(inputs)))
    left = jnp.concatenate([m.astype(bf16) for m in mixing], axis=1)
    right = jnp.concatenate(sources, axis=0)
    return dot(left, right)


def line_kernel(a_ref, w_ref, bias_ref, rate_ref, mask_ref, out_ref, coefs, steps, sums, ends, states, entering):
    length, expand = a_ref.shape
    chunks = length // CHUNK
    lane = lax.broadcasted_iota(jnp.int32, (CHUNK, LANES), 1)
    head = lax.broadcasted_iota(jnp.int32, (LANES, expand), 0)
    channel = lax.broadcasted_iota(jnp.int32, (LANES, expand), 1)
    spread = [
        (head == channel // 32 + 64 * d).astype(f32).astype(bf16) for d in range(2)
    ]
    w_proj = w_ref[...]
    for c in range(chunks):
        at = slice(c * CHUNK, (c + 1) * CHUNK)
        values = a_ref[at, :]
        k, s, q, end = chunk_terms(
            values, w_proj, bias_ref[...], rate_ref[...], mask_ref[...], c * CHUNK
        )
        coefs[at, :], steps[at, :], sums[at, :] = k, s, q
        ends[8 * c : 8 * c + 8, :] = jnp.broadcast_to(end, (8, LANES))
        tail = (jnp.exp2(jnp.where(lane < 64, q - end, -q)) * s).astype(bf16)
        wide = values.astype(f32)
        for d in range(2):
            if (c == chunks - 1, c == 0)[d]:
                continue
            weighted = (wide * dot(tail, spread[d])).astype(bf16)
            write = k[:, 64 * d + 32 : 64 * d + 48].astype(bf16)
            states[d, c] = dot(write, weighted, ((0,), (0,)))
    fade = jnp.exp2(-ends[...])
    high = fade.astype(bf16)
    low = (fade - high.astype(f32)).astype(bf16)
    for d in range(2):
        decay = dot(high, spread[d]) + dot(low, spread[d])
        order = range(chunks) if d == 0 else range(chunks - 1, -1, -1)
        running = None
        for c in order:
            if running is not None:
                entering[d, c] = running.astype(bf16)
            if c == order[-1]:
                break
            new = states[d, c]
            if running is not None:
                new = new + running * decay[8 * c : 8 * c + 1, :]
            running = new
    for c in range(chunks):
        at = slice(c * CHUNK, (c + 1) * CHUNK)
        values = a_ref[at, :]
        k, q = coefs[at, :], sums[at, :]
        end = ends[8 * c : 8 * c + 1, :]
        q_t, steps_t = q.T, steps[at, :].T
        weights = local_weights(k)
        head_in = jnp.exp2(jnp.where(lane < 64, -q, q - end)).astype(bf16)
        read = k.astype(bf16)
        for tile in range(expand // LANES):
            lanes = slice(tile * LANES, (tile + 1) * LANES)
            total = local_tile(values, tile, weights, q, q_t, steps_t)
            for d in range(2):
                if (c == 0, c == chunks - 1)[d]:
                    continue
                carried = dot(read[:, 64 * d + 48 : 64 * d + 64], entering[d, c, :, lanes])
                total = total + dot(head_in, spread[d][:, lanes]) * carried
            out_ref[at, lanes] = total.astype(bf16)


def swept_lines(values, gathered, bias, rate, mask):
    length, expand = values.shape
    chunks = length // CHUNK
    return pl.pallas_call(
        line_kernel,
        grid=(1,),
        in_specs=[
            pl.BlockSpec((length, expand), lambda i: (0, 0)),
            pl.BlockSpec((expand, LANES), lambda i: (0, 4)),
            pl.BlockSpec((1, LANES), lambda i: (0, 0)),
            pl.BlockSpec((1, LANES), lambda i: (0, 0)),
            pl.BlockSpec((1, LANES), lambda i: (0, 0)),
        ],
        out_specs=pl.BlockSpec((length, expand), lambda i: (0, 0)),
        out_shape=jax.ShapeDtypeStruct((length, expand), bf16),
        scratch_shapes=[
            pltpu.VMEM((length, LANES), f32),
            pltpu.VMEM((length, LANES), f32),
            pltpu.VMEM((length, LANES), f32),
            pltpu.VMEM((8 * chunks, LANES), f32),
            pltpu.VMEM((2, chunks, STATE, expand), f32),
            pltpu.VMEM((2, chunks, STATE, expand), bf16),
        ],
        compiler_params=pltpu.CompilerParams(vmem_limit_bytes=48 * 2**20),
        name="sweep_rows",
    )(values, gathered, bias, rate, mask)


def column_kernel(a_ref, w_ref, bias_ref, rate_ref, mask_ref, out_ref):
    sources, _, height, expand = a_ref.shape
    values = a_ref[...].reshape(CHUNK, expand)
    k, s, q, _ = chunk_terms(values, w_ref[...], bias_ref[...], rate_ref[...], mask_ref[...], 0)
    weights = local_weights(k)
    q_t, steps_t = q.T, s.T
    for tile in range(expand // LANES):
        lanes = slice(tile * LANES, (tile + 1) * LANES)
        total = local_tile(values, tile, weights, q, q_t, steps_t)
        out_ref[:, :, :, lanes] = total.astype(bf16).reshape(sources, 1, height, LANES)


def swept_columns(values, gathered, bias, rate, mask):
    sources, lines, height, expand = values.shape
    return pl.pallas_call(
        column_kernel,
        grid=(lines,),
        in_specs=[
            pl.BlockSpec((sources, 1, height, expand), lambda i: (0, i, 0, 0)),
            pl.BlockSpec((expand, LANES), lambda i: (0, 5)),
            pl.BlockSpec((1, LANES), lambda i: (0, 0)),
            pl.BlockSpec((1, LANES), lambda i: (0, 0)),
            pl.BlockSpec((1, LANES), lambda i: (0, 0)),
        ],
        out_specs=pl.BlockSpec((sources, 1, height, expand), lambda i: (0, i, 0, 0)),
        out_shape=jax.ShapeDtypeStruct(values.shape, bf16),
        compiler_params=pltpu.CompilerParams(vmem_limit_bytes=48 * 2**20),
        name="sweep_columns",
    )(values, gathered, bias, rate, mask)


def output_kernel(
    act_ref, rows_ref, columns_ref, x_ref, gain_ref, wg_ref, wo_ref, skip_ref, out_gain_ref, out_ref, *, height
):
    block, expand = act_ref.shape
    tokens = columns_ref.shape[0]
    breadth = tokens // height
    x = x_ref[...].astype(f32)
    normed = normalized(x, gain_ref[...]).astype(bf16)
    gating = dot(normed, wg_ref[...], ((1,), (1,))).astype(bf16).astype(f32)
    at = lax.broadcasted_iota(jnp.int32, (block, tokens), 0) + pl.program_id(0) * block
    source = lax.broadcasted_iota(jnp.int32, (block, tokens), 1)
    h, w = at // breadth, at % breadth
    back = (source == w * height + h).astype(f32).astype(bf16)
    summed = (
        dot(back, columns_ref[...])
        + rows_ref[...].astype(f32)
        + skip_ref[...] * act_ref[...].astype(f32)
    )
    gate = gating / (1.0 + jnp.exp(-gating))
    mixed = (normalized(summed, out_gain_ref[...]) * gate).astype(bf16)
    out_ref[...] = (x + dot(mixed, wo_ref[...])).astype(bf16)


def projected(act, rows, columns, x, gain, w_in, gathered, skip, out_gain, height):
    tokens, expand = act.shape
    channels = x.shape[1]
    block = 128
    one = lambda i: (0, 0)
    return pl.pallas_call(
        functools.partial(output_kernel, height=height),
        grid=(tokens // block,),
        in_specs=[
            pl.BlockSpec((block, expand), lambda i: (i, 0)),
            pl.BlockSpec((block, expand), lambda i: (i, 0)),
            pl.BlockSpec((tokens, expand), one),
            pl.BlockSpec((block, channels), lambda i: (i, 0)),
            pl.BlockSpec((1, channels), one),
            pl.BlockSpec((expand, channels), lambda i: (1, 0)),
            pl.BlockSpec((expand, channels), one),
            pl.BlockSpec((1, expand), one),
            pl.BlockSpec((1, expand), one),
        ],
        out_specs=pl.BlockSpec((block, channels), lambda i: (i, 0)),
        out_shape=jax.ShapeDtypeStruct((tokens, channels), bf16),
        compiler_params=pltpu.CompilerParams(vmem_limit_bytes=48 * 2**20),
        name="gate_and_project",
    )(act, rows, columns, x, gain, w_in, gathered, skip, out_gain)


def head_lanes(pair):
    gap = jnp.zeros((2, 64 - HEADS), f32)
    return jnp.concatenate([pair, gap], axis=1).reshape(1, LANES)


def on_device(
    tokens, tile_mask, norm_gain, w_in, conv_weight, conv_bias, w_proj, dt_bias, decay_rate, skip_gain, out_gain, w_out
):
    both = ("row", "col")
    count_row, count_col = lax.axis_size("row"), lax.axis_size("col")
    row, col = lax.axis_index("row"), lax.axis_index("col")
    height, breadth, channels = tokens.shape
    local = height * breadth
    expand = conv_bias.shape[0]
    devices = count_row * count_col

    flags = jnp.broadcast_to(
        jnp.pad(tile_mask.reshape(1, -1).astype(bf16), ((0, 0), (0, LANES - tile_mask.size))),
        (w_out.shape[0], LANES),
    )
    gathered = lax.all_gather(
        jnp.concatenate([w_out, w_proj, flags], axis=1), both, axis=0, tiled=True
    )

    own = w_in.T
    weights = lax.all_to_all(
        jnp.broadcast_to(own[None], (devices,) + own.shape), both, 0, 0, tiled=True
    ).reshape(2 * expand, channels)

    above, below = shifted(tokens[-1:], "row", 1), shifted(tokens[:1], "row", -1)
    tall = jnp.concatenate([above, tokens, below], axis=0)
    before, after = shifted(tall[:, -1:], "col", 1), shifted(tall[:, :1], "col", -1)
    after_last = jnp.concatenate([jnp.zeros_like(after[:1]), after], axis=0)
    body = jnp.concatenate(
        [after_last[:-1], jnp.zeros((height + 2, 6, channels), bf16), before, tall], axis=1
    ).reshape((height + 2) * STRIDE, channels)
    x_ext = jnp.concatenate([body, after_last[-1], jnp.zeros((15, channels), bf16)], axis=0)

    act, turned = filtered(
        x_ext,
        norm_gain.reshape(1, -1),
        weights,
        conv_weight,
        conv_bias.reshape(1, -1),
        local,
    )

    marks = gathered[:: w_out.shape[0], channels + w_proj.shape[1] :][:, :2].astype(f32)
    marks = marks.reshape(count_row, count_col, 2)
    line = row * height + col
    mask_line = lax.dynamic_slice_in_dim(
        marks.transpose(0, 2, 1).reshape(2 * count_row, count_col), line // TILE, 1, axis=0
    )
    mask_line = jnp.pad(mask_line, ((0, 0), (0, LANES - count_col)))
    mask_column = lax.dynamic_slice_in_dim(marks, col, 1, axis=1).reshape(1, 2 * count_row)
    mask_column = jnp.pad(mask_column, ((0, 0), (0, LANES - 2 * count_row)))
    rate = decay_rate * LOG2E

    lines = lax.all_to_all(
        act.reshape(height, breadth, expand), "col", 0, 0, tiled=True
    ).reshape(count_col * breadth, expand)
    rows_out = swept_lines(
        lines, gathered, head_lanes(dt_bias[:2]), head_lanes(rate[:2]), mask_line
    )
    rows_back = lax.all_to_all(
        rows_out.reshape(count_col, breadth, expand), "col", 0, 0, tiled=True
    ).reshape(local, expand)

    columns = lax.all_to_all(
        turned.reshape(count_row, breadth // count_row * height, expand), "row", 0, 0, tiled=True
    ).reshape(count_row, breadth // count_row, height, expand)
    columns_out = swept_columns(
        columns, gathered, head_lanes(dt_bias[2:]), head_lanes(rate[2:]), mask_column
    )
    columns_back = lax.all_to_all(
        columns_out.reshape(count_row, breadth // count_row * height, expand),
        "row",
        0,
        0,
        tiled=True,
    ).reshape(local, expand)

    result = projected(
        act,
        rows_back,
        columns_back,
        tokens.reshape(local, channels),
        norm_gain.reshape(1, -1),
        weights,
        gathered,
        skip_gain.reshape(1, -1),
        out_gain.reshape(1, -1),
        height,
    )
    return result.reshape(height, breadth, channels)


def solution(mesh):
    placed = (
        P("row", "col", None),
        P("row", "col"),
        P(),
        P(None, ("row", "col")),
        P(),
        P(),
        P(("row", "col"), None),
        P(),
        P(),
        P(),
        P(),
        P(("row", "col"), None),
    )
    return jax.shard_map(
        on_device, mesh=mesh, in_specs=placed, out_specs=P("row", "col", None), check_vma=False
    )
```

```python
import functools

import jax
import jax.numpy as jnp
from jax import lax
from jax.experimental import pallas as pl
from jax.experimental.pallas import tpu as pltpu
from jax.sharding import Mesh, PartitionSpec as P

STATE = 16
HEADS = 32
TILE = 16
CHUNK = 128
LANES = 128
STRIDE = 24
LOG2E = 1.4426950408889634
GRANT = 56 * 2**20

f32 = jnp.float32
bf16 = jnp.bfloat16


def dot(a, b, contract=((1,), (0,))):
    return lax.dot_general(a, b, (contract, ((), ())), preferred_element_type=f32)


def shifted(x, axis, step):
    count = lax.axis_size(axis)
    pairs = [(i, i + step) for i in range(count) if 0 <= i + step < count]
    return lax.ppermute(x, axis, pairs)


def diagonal(x, down, right):
    axes = ("row", "chip", "core")
    rows, columns = lax.axis_size("row"), lax.axis_size(("chip", "core"))
    pairs = [
        (r * columns + c, (r + down) * columns + c + right)
        for r in range(rows)
        for c in range(columns)
        if 0 <= r + down < rows and 0 <= c + right < columns
    ]
    return lax.ppermute(x, axes, pairs)


def here():
    return lax.axis_index("row"), 2 * lax.axis_index("chip") + lax.axis_index("core")


def normalized(x, gain):
    average = jnp.mean(x, axis=-1, keepdims=True)
    centered = x - average
    spread = jnp.mean(centered * centered, axis=-1, keepdims=True)
    return centered * lax.rsqrt(spread + 1e-05) * gain


def paired(own_ref, other_ref, core):
    own, other = own_ref[...].astype(f32), other_ref[...].astype(f32)
    return jnp.where(core == 0, own, other), jnp.where(core == 0, other, own)


def rows_of_eight(*pieces):
    count = pieces[0].shape[0] // 8
    parts = [p.reshape(count, 8, p.shape[1]) for p in pieces]
    return jnp.concatenate(parts, axis=1).reshape(-1, pieces[0].shape[1]).astype(bf16)


def input_weights(own_ref, other_ref, core):
    half = own_ref.shape[1] // 2
    even, odd = paired(own_ref, other_ref, core)
    return rows_of_eight(even[:, :half], even[:, half:], odd[:, :half], odd[:, half:])


def parcel_kernel(mask, in_ref, out_ref, proj_ref, parcel_ref):
    place = here()
    row = lax.broadcasted_iota(jnp.int32, (8, LANES), 0)
    lane = lax.broadcasted_iota(jnp.int32, (8, LANES), 1)
    flags = jnp.zeros((8, LANES), f32)
    for i in range(mask.shape[1]):
        flags = jnp.where(
            (row == i) & (lane == place[1]), mask[:, i : i + 1].astype(f32), flags
        )
    turned = in_ref[...].astype(f32)
    parts = [turned[:8], turned[8:], out_ref[...].astype(f32), proj_ref[...].astype(f32), flags]
    at = 0
    for part in parts:
        width = part.shape[1]
        parcel_ref[:, :, at : at + width] = jnp.broadcast_to(
            part.astype(bf16)[None], (parcel_ref.shape[0], 8, width)
        )
        at += width


def parcels(mask, turned, w_out, w_proj, groups):
    width = 2 * turned.shape[1] + w_out.shape[1] + w_proj.shape[1] + LANES
    block = 16
    one = lambda i: (0, 0)
    return pl.pallas_call(
        parcel_kernel,
        grid=(groups // block,),
        in_specs=[
            pl.BlockSpec(mask.shape, one),
            pl.BlockSpec(turned.shape, one),
            pl.BlockSpec(w_out.shape, one),
            pl.BlockSpec(w_proj.shape, one),
        ],
        out_specs=pl.BlockSpec((block, 8, width), lambda i: (i, 0, 0)),
        out_shape=jax.ShapeDtypeStruct((groups, 8, width), bf16),
        compiler_params=pltpu.CompilerParams(vmem_limit_bytes=GRANT),
        name="parcels",
    )(mask, turned, w_out, w_proj)


def filter_kernel(
    x_ref, gain_ref, own_ref, other_ref, taps_ref, bias_ref, act_ref, turned_ref, normed, branch, order
):
    place = here()
    padded = x_ref.shape[0]
    tokens, width = act_ref.shape
    height = padded // STRIDE - 2
    breadth = tokens // height

    @pl.when(pl.program_id(0) == 0)
    def _():
        step = 64
        for at in range(0, padded, step):
            x = x_ref[at : at + step, :].astype(f32)
            normed[at : at + step, :] = normalized(x, gain_ref[...]).astype(bf16)
        to = lax.broadcasted_iota(jnp.int32, (tokens, tokens), 0)
        source = lax.broadcasted_iota(jnp.int32, (tokens, tokens), 1)
        w, h = to // height, to % height
        order[...] = (source == h * breadth + w).astype(f32).astype(bf16)

    weights = input_weights(own_ref, other_ref, place[1] % 2)
    product = dot(normed[...], weights, ((1,), (1,)))
    branch[...] = product.astype(bf16).astype(f32)
    rows = 4
    span = rows * STRIDE + 8
    for lane in range(0, width, LANES):
        lanes = slice(lane, lane + LANES)
        taps = [taps_ref[k : k + 1, lanes] for k in range(9)]
        for h in range(0, height, rows):
            windows = [
                branch[(h + i) * STRIDE : (h + i) * STRIDE + span, lanes] for i in range(3)
            ]
            left, middle, right = [
                windows[0] * taps[j] + windows[1] * taps[3 + j] + windows[2] * taps[6 + j]
                for j in range(3)
            ]
            convolved = (
                middle
                + pltpu.roll(left, 1, 0)
                + pltpu.roll(right, span - 1, 0)
                + bias_ref[:, lanes]
            )
            activated = convolved / (1.0 + jnp.exp(-convolved))
            kept = activated[: rows * STRIDE].reshape(rows, STRIDE, LANES)[:, 8:, :]
            act_ref[h * breadth : (h + rows) * breadth, lanes] = kept.reshape(
                rows * breadth, LANES
            ).astype(bf16)
    turned_ref[...] = dot(order[...], act_ref[...]).astype(bf16)


def filtered(x, gain, own, other, taps, bias, tokens):
    expand = bias.shape[1]
    padded, channels = x.shape
    width = 256
    piece = pl.BlockSpec((width // 4, 2 * channels), lambda c: (c, 0))
    return pl.pallas_call(
        filter_kernel,
        grid=(expand // width,),
        in_specs=[
            pl.BlockSpec((padded, channels), lambda c: (0, 0)),
            pl.BlockSpec((1, channels), lambda c: (0, 0)),
            piece,
            piece,
            pl.BlockSpec((9, width), lambda c: (0, c)),
            pl.BlockSpec((1, width), lambda c: (0, c)),
        ],
        out_specs=[pl.BlockSpec((tokens, width), lambda c: (0, c))] * 2,
        out_shape=[jax.ShapeDtypeStruct((tokens, expand), bf16)] * 2,
        scratch_shapes=[
            pltpu.VMEM((padded, channels), bf16),
            pltpu.VMEM((padded, width), f32),
            pltpu.VMEM((tokens, tokens), bf16),
        ],
        compiler_params=pltpu.CompilerParams(vmem_limit_bytes=GRANT),
        cost_estimate=pl.CostEstimate(
            flops=2 * padded * channels * expand, bytes_accessed=6 * 2**20, transcendentals=tokens * expand
        ),
        name="norm_project_filter",
    )(x, gain, own, other, taps, bias)


def head_lanes(ref, first):
    heads = ref.shape[1]
    head = lax.broadcasted_iota(jnp.int32, (heads, LANES), 0)
    lane = lax.broadcasted_iota(jnp.int32, (heads, LANES), 1)
    placed = [
        lax.dot_general(
            ref[...],
            (lane == head + 64 * d).astype(f32),
            (((1,), (0,)), ((), ())),
            precision=lax.Precision.HIGHEST,
            preferred_element_type=f32,
        )
        for d in range(2)
    ]
    return placed[0][first : first + 1] + placed[1][first + 1 : first + 2]


def chunk_terms(values, w_proj, bias, rate, kept):
    coefs = dot(values, w_proj)
    at = lax.broadcasted_iota(jnp.int32, (CHUNK, LANES), 0)
    lane = lax.broadcasted_iota(jnp.int32, (CHUNK, LANES), 1)
    v = coefs + bias
    steps = kept * (jnp.maximum(v, 0.0) + jnp.log1p(jnp.exp(-jnp.abs(v))))
    decays = steps * rate
    lower = (lane <= at).astype(f32).astype(bf16)
    high = decays.astype(bf16)
    rest = decays - high.astype(f32)
    middle = rest.astype(bf16)
    low = (rest - middle.astype(f32)).astype(bf16)
    total = dot(lower, high) + (dot(lower, middle) + dot(lower, low))
    sums = jnp.where(lane < 64, total, total - decays)
    return coefs, steps, sums, total[CHUNK - 1 :, :]


def local_weights(coefs, span):
    at = lax.broadcasted_iota(jnp.int32, (CHUNK, CHUNK), 0)
    source = lax.broadcasted_iota(jnp.int32, (CHUNK, CHUNK), 1)
    c = coefs.astype(bf16)
    forward = dot(c[:, 48:64], c[:, 32:48], ((1,), (1,)))
    backward = dot(c[:, 112:128], c[:, 96:112], ((1,), (1,)))
    together = source // span == at // span
    return (
        source <= at,
        jnp.where((source <= at) & together, forward, 0.0).astype(bf16),
        jnp.where((source >= at) & together, backward, 0.0).astype(bf16),
    )


def local_tile(values, tile, weights, sums, sums_t, steps_t):
    causal, forward, backward = weights
    lane = lax.broadcasted_iota(jnp.int32, (CHUNK, LANES), 1)
    inputs = values[:, tile * LANES : (tile + 1) * LANES]
    mixing, sources = [], []
    for k in range(4):
        j = 4 * tile + k
        exponent = jnp.where(
            causal,
            sums_t[j : j + 1, :] - sums[:, j : j + 1],
            sums[:, 64 + j : 65 + j] - sums_t[64 + j : 65 + j, :],
        )
        scale = forward * steps_t[j : j + 1, :] + backward * steps_t[64 + j : 65 + j, :]
        mixing.append(jnp.exp2(exponent.astype(bf16)) * scale)
        sources.append(jnp.where(lane // 32 == k, inputs, jnp.zeros_like(inputs)))
    left = jnp.concatenate(mixing, axis=1)
    right = jnp.concatenate(sources, axis=0)
    return dot(left, right)


def line_kernel(
    a_ref, own_ref, other_ref, own_flags, other_flags, bias_ref, rate_ref, out_ref, coefs, steps, sums, ends, states, entering
):
    place = here()
    length, expand = a_ref.shape
    chunks = length // CHUNK
    lane = lax.broadcasted_iota(jnp.int32, (CHUNK, LANES), 1)
    spread = head_spread(expand)
    w_proj = rows_of_eight(*paired(own_ref, other_ref, place[1] % 2))
    bias, rate = head_lanes(bias_ref, 0), head_lanes(rate_ref, 0) * LOG2E
    flags = own_flags[...].astype(f32) + other_flags[...].astype(f32)
    line = lax.broadcasted_iota(jnp.int32, flags.shape, 0)
    mine = (line // (flags.shape[0] // 4) == place[0]) & (line % 8 == place[1] // TILE)
    mask = jnp.sum(jnp.where(mine, flags, 0.0), axis=0, keepdims=True)
    position = lax.broadcasted_iota(jnp.int32, (CHUNK, LANES), 0)
    for c in range(chunks):
        tile_at = lane == (position + c * CHUNK) // TILE
        kept = jnp.sum(jnp.where(tile_at, mask, 0.0), axis=1, keepdims=True)
        at = slice(c * CHUNK, (c + 1) * CHUNK)
        values = a_ref[at, :]
        k, s, q, end = chunk_terms(values, w_proj, bias, rate, kept)
        coefs[at, :], steps[at, :], sums[at, :] = k, s, q
        ends[8 * c : 8 * c + 8, :] = jnp.broadcast_to(end, (8, LANES))
        tail = (jnp.exp2(jnp.where(lane < 64, q - end, -q)) * s).astype(bf16)
        wide = values.astype(f32)
        for d in range(2):
            if (c == chunks - 1, c == 0)[d]:
                continue
            weighted = (wide * dot(tail, spread[d])).astype(bf16)
            write = k[:, 64 * d + 32 : 64 * d + 48].astype(bf16)
            states[d, c] = dot(write, weighted, ((0,), (0,)))
    fade = jnp.exp2(-ends[...])
    high = fade.astype(bf16)
    low = (fade - high.astype(f32)).astype(bf16)
    for d in range(2):
        decay = dot(high, spread[d]) + dot(low, spread[d])
        order = range(chunks) if d == 0 else range(chunks - 1, -1, -1)
        running = None
        for c in order:
            if running is not None:
                entering[d, c] = running.astype(bf16)
            if c == order[-1]:
                break
            new = states[d, c]
            if running is not None:
                new = new + running * decay[8 * c : 8 * c + 1, :]
            running = new
    for c in range(chunks):
        at = slice(c * CHUNK, (c + 1) * CHUNK)
        values = a_ref[at, :]
        k, q = coefs[at, :], sums[at, :]
        end = ends[8 * c : 8 * c + 1, :]
        q_t, steps_t = q.T, steps[at, :].T.astype(bf16)
        weights = local_weights(k, CHUNK)
        head_in = jnp.exp2(jnp.where(lane < 64, -q, q - end)).astype(bf16)
        read = k.astype(bf16)
        for tile in range(expand // LANES):
            lanes = slice(tile * LANES, (tile + 1) * LANES)
            total = local_tile(values, tile, weights, q, q_t, steps_t)
            for d in range(2):
                if (c == 0, c == chunks - 1)[d]:
                    continue
                carried = dot(read[:, 64 * d + 48 : 64 * d + 64], entering[d, c, :, lanes])
                total = total + dot(head_in, spread[d][:, lanes]) * carried
            out_ref[at, lanes] = total.astype(bf16)


def piece_specs(rows, *columns):
    return [pl.BlockSpec((rows, LANES), lambda i, c=c: (0, c)) for c in columns for _ in range(2)]


def swept_lines(values, own, other, bias, rate):
    length, expand = values.shape
    chunks = length // CHUNK
    small = pl.BlockSpec(bias.shape, lambda i: (0, 0))
    return pl.pallas_call(
        line_kernel,
        grid=(1,),
        in_specs=[
            pl.BlockSpec((length, expand), lambda i: (0, 0)),
            *piece_specs(own.shape[0], 12, 14),
            small,
            small,
        ],
        out_specs=pl.BlockSpec((length, expand), lambda i: (0, 0)),
        out_shape=jax.ShapeDtypeStruct((length, expand), bf16),
        scratch_shapes=[
            pltpu.VMEM((length, LANES), f32),
            pltpu.VMEM((length, LANES), f32),
            pltpu.VMEM((length, LANES), f32),
            pltpu.VMEM((8 * chunks, LANES), f32),
            pltpu.VMEM((2, chunks, STATE, expand), f32),
            pltpu.VMEM((2, chunks, STATE, expand), bf16),
        ],
        compiler_params=pltpu.CompilerParams(vmem_limit_bytes=GRANT),
        cost_estimate=pl.CostEstimate(
            flops=6 * 2**30, bytes_accessed=3 * 2**20, transcendentals=2**21
        ),
        name="sweep_rows",
    )(values, own, other, own, other, bias, rate)


def head_spread(expand):
    head = lax.broadcasted_iota(jnp.int32, (LANES, expand), 0)
    channel = lax.broadcasted_iota(jnp.int32, (LANES, expand), 1)
    return [(head == channel // 32 + 64 * d).astype(f32).astype(bf16) for d in range(2)]


def by_line(coefs, first, height):
    lines = CHUNK // height
    lane = lax.broadcasted_iota(jnp.int32, (LANES, lines * STATE), 0)
    to = lax.broadcasted_iota(jnp.int32, (LANES, lines * STATE), 1)
    copied = dot(coefs, (lane == first + to % STATE).astype(f32).astype(bf16))
    at = lax.broadcasted_iota(jnp.int32, copied.shape, 0)
    place = lax.broadcasted_iota(jnp.int32, copied.shape, 1)
    return jnp.where(at // height == place // STATE, copied, 0.0).astype(bf16)


def column_kernel(
    a_ref, own_ref, other_ref, own_flags, other_flags, bias_ref, rate_ref, coefs_ref, steps_ref, sums_ref, read_ref, *refs
):
    place = here()
    slots = len(refs) - 5
    slot_refs, (proj, kept_lanes, heads, spread, decays) = refs[:slots], refs[slots:]
    expand = a_ref.shape[1]
    groups = slots + 1
    states = slot_refs[0].shape[0] - 16
    group = pl.program_id(0)
    part = states // pl.num_programs(0)
    lines = part // STATE
    height = CHUNK // lines
    lane = lax.broadcasted_iota(jnp.int32, (CHUNK, LANES), 1)

    @pl.when(group == 0)
    def _():
        flags = (own_flags[...].astype(f32) + other_flags[...].astype(f32)).astype(bf16)
        to = lax.broadcasted_iota(jnp.int32, (CHUNK, flags.shape[0]), 0)
        source = lax.broadcasted_iota(jnp.int32, (CHUNK, flags.shape[0]), 1)
        mine = (source // (flags.shape[0] // groups) == place[0]) & (
            source % 8 == to % height // TILE
        )
        marks = dot(mine.astype(f32).astype(bf16), flags)
        kept = jnp.sum(jnp.where(lane == place[1], marks, 0.0), axis=1, keepdims=True)
        kept_lanes[...] = jnp.broadcast_to(kept, kept_lanes.shape)
        proj[...] = rows_of_eight(*paired(own_ref, other_ref, place[1] % 2))
        heads[0:1, :] = head_lanes(bias_ref, 2)
        heads[1:2, :] = head_lanes(rate_ref, 2) * LOG2E
        for d, matrix in enumerate(head_spread(expand)):
            spread[d] = matrix

    values = a_ref[...]
    k, s, q, _ = chunk_terms(values, proj[...], heads[0:1, :], heads[1:2, :], kept_lanes[...])
    coefs_ref[...], steps_ref[...], sums_ref[...] = k, s, q

    inclusive = q + jnp.where(lane < 64, 0.0, s * heads[1:2, :])
    starts, ends = [jnp.zeros((1, LANES), f32)], []
    for line in range(lines):
        ends.append(inclusive[(line + 1) * height - 1 : (line + 1) * height, :])
        starts.append(ends[-1])
    wide = lambda rows: jnp.concatenate(
        [jnp.broadcast_to(r, (height, LANES)) for r in rows], axis=0
    )
    start, end = wide(starts[:lines]), wide(ends)
    tail = (jnp.exp2(jnp.where(lane < 64, q - end, start - q)) * s).astype(bf16)
    enter = jnp.exp2(jnp.where(lane < 64, start - q, q - end))
    is_read = (lane % 64) >= 48
    read_ref[...] = jnp.where(is_read, k, enter).astype(bf16)
    fade = jnp.exp2(
        jnp.concatenate([a - b for a, b in zip(starts[:lines], ends)] + [jnp.zeros((8 - lines, LANES), f32)], axis=0)
    )
    high = fade.astype(bf16)
    low = (fade - high.astype(f32)).astype(bf16)
    writes = k.astype(bf16)
    inputs = values.astype(f32)
    totals, fades = [], []
    for d in range(2):
        weighted = (inputs * dot(tail, spread[d])).astype(bf16)
        write = by_line(writes, 64 * d + 32, height)
        totals.append(dot(write, weighted, ((0,), (0,))).astype(bf16))
        fades.append(dot(high, spread[d]) + dot(low, spread[d]))
    at = pl.ds(pl.multiple_of(group * part, part), part)
    for d, ref in enumerate(slot_refs):
        onward = place[0] + d + 1 < groups

        @pl.when(onward)
        def _():
            ref[at, :] = totals[0]
            decays[d, pl.ds(pl.multiple_of(group * 8, 8), 8), :] = fades[0]

        @pl.when(jnp.logical_not(onward))
        def _():
            ref[at, :] = totals[1]
            decays[d, pl.ds(pl.multiple_of(group * 8, 8), 8), :] = fades[1]

    @pl.when(group == pl.num_programs(0) - 1)
    def _():
        for d, ref in enumerate(slot_refs):
            rows = [decays[d, 8 * g : 8 * g + lines, :] for g in range(states // part)]
            ref[states:, :] = jnp.concatenate(rows, axis=0).astype(bf16)


def column_states(values, own, other, bias, rate, height, slots):
    tokens, expand = values.shape
    groups = tokens // CHUNK
    states = tokens // height * STATE
    small = pl.BlockSpec(bias.shape, lambda i: (0, 0))
    block = pl.BlockSpec((CHUNK, expand), lambda i: (i, 0))
    thin = pl.BlockSpec((CHUNK, LANES), lambda i: (i, 0))
    return pl.pallas_call(
        column_kernel,
        grid=(groups,),
        in_specs=[block, *piece_specs(own.shape[0], 13, 14), small, small],
        out_specs=[thin] * 4
        + [pl.BlockSpec((states + 16, expand), lambda i: (0, 0))] * (slots - 1),
        out_shape=[jax.ShapeDtypeStruct((tokens, LANES), f32)] * 3
        + [jax.ShapeDtypeStruct((tokens, LANES), bf16)]
        + [jax.ShapeDtypeStruct((states + 16, expand), bf16)] * (slots - 1),
        scratch_shapes=[
            pltpu.VMEM((expand, LANES), bf16),
            pltpu.VMEM((CHUNK, LANES), f32),
            pltpu.VMEM((8, LANES), f32),
            pltpu.VMEM((2, LANES, expand), bf16),
            pltpu.VMEM((slots - 1, 8 * groups, expand), f32),
        ],
        compiler_params=pltpu.CompilerParams(vmem_limit_bytes=GRANT),
        cost_estimate=pl.CostEstimate(
            flops=2**31, bytes_accessed=3 * 2**20, transcendentals=2**18
        ),
        name="column_states",
    )(values, own, other, own, other, bias, rate)


def mix_kernel(a_ref, coefs_ref, steps_ref, sums_ref, out_ref, *, height):
    values = a_ref[...]
    q = sums_ref[...]
    weights = local_weights(coefs_ref[...], height)
    q_t, steps_t = q.T, steps_ref[...].T.astype(bf16)
    for tile in range(a_ref.shape[1] // LANES):
        lanes = slice(tile * LANES, (tile + 1) * LANES)
        out_ref[:, lanes] = local_tile(values, tile, weights, q, q_t, steps_t).astype(bf16)


def mixed_columns(values, coefs, steps, sums, height):
    tokens, expand = values.shape
    block = pl.BlockSpec((CHUNK, expand), lambda i: (i, 0))
    thin = pl.BlockSpec((CHUNK, LANES), lambda i: (i, 0))
    return pl.pallas_call(
        functools.partial(mix_kernel, height=height),
        grid=(tokens // CHUNK,),
        in_specs=[block, thin, thin, thin],
        out_specs=block,
        out_shape=jax.ShapeDtypeStruct((tokens, expand), bf16),
        compiler_params=pltpu.CompilerParams(vmem_limit_bytes=GRANT),
        cost_estimate=pl.CostEstimate(
            flops=2**32, bytes_accessed=3 * 2**20, transcendentals=2**21
        ),
        name="mix_columns",
    )(values, coefs, steps, sums)


def entering_kernel(
    local_ref, read_ref, act_ref, skip_ref, x_ref, gain_ref, own_gate, other_gate, own_out, other_out, *refs
):
    place = here()
    slots = len(refs) - 5
    slot_refs, (part_ref, gate_ref, w_out_ref, w_gate, columns) = refs[:slots], refs[slots:]
    expand = local_ref.shape[1]
    states = slot_refs[0].shape[0] - 16
    groups = local_ref.shape[0] // CHUNK
    part = states // groups
    lines = part // STATE
    height = CHUNK // lines
    spread = head_spread(expand)
    row = place[0]
    decays = [ref[states:, :].astype(f32) for ref in slot_refs]
    for g in range(groups):
        at = slice(g * CHUNK, (g + 1) * CHUNK)
        total = local_ref[at, :].astype(f32)
        read = read_ref[at, :]
        for d in range(2):
            order = range(slots) if d == 0 else range(slots - 1, -1, -1)
            entering, product = [], [None] * lines
            sums = [jnp.zeros((STATE, expand), f32)] * lines
            for step, k in enumerate(order):
                reaches = row > step if d == 0 else row + step + 1 <= slots
                for line in range(lines):
                    at_state = g * part + line * STATE
                    state = slot_refs[k][at_state : at_state + STATE, :].astype(f32)
                    if product[line] is not None:
                        state = state * product[line]
                    sums[line] = sums[line] + jnp.where(reaches, state, 0.0)
                    fade = decays[k][g * lines + line : g * lines + line + 1, :]
                    product[line] = fade if product[line] is None else product[line] * fade
            entering = jnp.concatenate(sums, axis=0).astype(bf16)
            carried = dot(by_line(read, 64 * d + 48, height), entering)
            total = total + dot(read, spread[d]) * carried
        columns[at, :] = total.astype(bf16)
    w_gate[...] = input_weights(own_gate, other_gate, place[1] % 2)
    w_out_ref[...] = rows_of_eight(*paired(own_out, other_out, place[1] % 2))
    tokens = local_ref.shape[0]
    breadth = tokens // height
    for g in range(groups):
        at = slice(g * CHUNK, (g + 1) * CHUNK)
        to = lax.broadcasted_iota(jnp.int32, (CHUNK, tokens), 0) + g * CHUNK
        source = lax.broadcasted_iota(jnp.int32, (CHUNK, tokens), 1)
        w, h = source // height, source % height
        back = (to == h * breadth + w).astype(f32).astype(bf16)
        direct = skip_ref[...] * act_ref[at, :].astype(f32)
        part_ref[at, :] = dot(back, columns[...]) + direct
        normed = normalized(x_ref[at, :].astype(f32), gain_ref[...]).astype(bf16)
        gating = dot(normed, w_gate[...], ((1,), (1,))).astype(bf16).astype(f32)
        gate_ref[at, :] = gating / (1.0 + jnp.exp(-gating))


def entered(local, read, act, skip, x, gain, own, other, slots):
    tokens, expand = local.shape
    pairs, channels = own.shape[0], x.shape[1]
    whole = lambda x: pl.BlockSpec(x.shape, lambda i: (0, 0))
    gate = pl.BlockSpec((pairs // 2, 2 * channels), lambda i: (1, 0))
    last = pl.BlockSpec((pairs, channels), lambda i: (0, 2))
    shapes = [
        jax.ShapeDtypeStruct((tokens, expand), f32),
        jax.ShapeDtypeStruct((tokens, expand), f32),
        jax.ShapeDtypeStruct((expand, channels), bf16),
    ]
    return pl.pallas_call(
        entering_kernel,
        grid=(1,),
        in_specs=[whole(a) for a in (local, read, act, skip, x, gain)]
        + [gate, gate, last, last]
        + [whole(a) for a in slots],
        out_specs=[whole(a) for a in shapes],
        out_shape=shapes,
        scratch_shapes=[
            pltpu.VMEM((expand, channels), bf16),
            pltpu.VMEM((tokens, expand), bf16),
        ],
        compiler_params=pltpu.CompilerParams(vmem_limit_bytes=GRANT),
        cost_estimate=pl.CostEstimate(
            flops=2**32, bytes_accessed=12 * 2**20, transcendentals=2**19
        ),
        name="enter_columns",
    )(local, read, act, skip, x, gain, own, other, own, other, *slots)


def output_kernel(part_ref, gate_ref, rows_ref, x_ref, w_ref, out_gain_ref, out_ref):
    summed = part_ref[...] + rows_ref[...].astype(f32)
    mixed = (normalized(summed, out_gain_ref[...]) * gate_ref[...]).astype(bf16)
    out_ref[...] = (x_ref[...].astype(f32) + dot(mixed, w_ref[...])).astype(bf16)


def projected(part, gate, rows, x, w_out, out_gain):
    tokens, expand = part.shape
    channels = x.shape[1]
    block = 128
    one = lambda i: (0, 0)
    wide = pl.BlockSpec((block, expand), lambda i: (i, 0))
    narrow = pl.BlockSpec((block, channels), lambda i: (i, 0))
    return pl.pallas_call(
        output_kernel,
        grid=(tokens // block,),
        in_specs=[
            wide,
            wide,
            wide,
            narrow,
            pl.BlockSpec((expand, channels), one),
            pl.BlockSpec((1, expand), one),
        ],
        out_specs=narrow,
        out_shape=jax.ShapeDtypeStruct((tokens, channels), bf16),
        compiler_params=pltpu.CompilerParams(vmem_limit_bytes=GRANT),
        name="gate_and_project",
    )(part, gate, rows, x, w_out, out_gain)


def on_device(
    tokens, tile_mask, norm_gain, w_in, conv_weight, conv_bias, w_proj, dt_bias, decay_rate, skip_gain, out_gain, w_out
):
    wide = ("chip", "core")
    count_row, count_chip = lax.axis_size("row"), lax.axis_size("chip")
    height, breadth, channels = tokens.shape
    local = height * breadth
    expand = conv_bias.shape[0]

    groups = count_row * count_chip
    parcel = parcels(tile_mask.T, w_in.T, w_out, w_proj, groups)
    own = lax.all_to_all(parcel, ("row", "chip"), 0, 0, tiled=True)
    above, below = shifted(tokens[-1:], "row", 1), shifted(tokens[:1], "row", -1)
    tall = jnp.concatenate([above, tokens, below], axis=0)
    before, after = [
        jnp.concatenate(
            [
                diagonal(tokens[-1:, edge], 1, step),
                shifted(tokens[:, edge], wide, step),
                diagonal(tokens[:1, edge], -1, step),
            ],
            axis=0,
        )
        for edge, step in ((slice(breadth - 1, breadth), 1), (slice(0, 1), -1))
    ]
    after_last = jnp.concatenate([jnp.zeros_like(after[:1]), after], axis=0)
    body = jnp.concatenate(
        [after_last[:-1], jnp.zeros((height + 2, 6, channels), bf16), before, tall], axis=1
    ).reshape((height + 2) * STRIDE, channels)
    x_ext = jnp.concatenate([body, after_last[-1], jnp.zeros((15, channels), bf16)], axis=0)

    own, x_ext = lax.optimization_barrier((own, x_ext))
    other = lax.ppermute(own, "core", [(0, 1), (1, 0)])
    own, other = [p.reshape(groups * 8, p.shape[2]) for p in (own, other)]

    act, turned = filtered(
        x_ext,
        norm_gain.reshape(1, -1),
        own,
        other,
        conv_weight,
        conv_bias.reshape(1, -1),
        local,
    )
    def spun(piece, d):
        return lax.ppermute(piece, "row", [(i, (i + d) % count_row) for i in range(count_row)])

    def dealt(x):
        return lax.all_to_all(
            x.reshape(-1, breadth, expand), wide, 0, 0, tiled=True
        ).reshape(-1, expand)

    lines = dealt(act)
    coefs, steps, sums, read, *states = column_states(
        turned, own, other, dt_bias, decay_rate, height, count_row
    )
    received = [spun(piece, d + 1) for d, piece in enumerate(states)]
    columns_local = mixed_columns(turned, coefs, steps, sums, height)
    lines, columns_local = lax.optimization_barrier((lines, columns_local))
    rows_out = swept_lines(lines, own, other, dt_bias, decay_rate)
    rows_out, received = lax.optimization_barrier((rows_out, received))
    rows_back = dealt(rows_out)
    x = tokens.reshape(local, channels)
    part, gate, full_out = entered(
        columns_local,
        read,
        act,
        skip_gain.reshape(1, -1),
        x,
        norm_gain.reshape(1, -1),
        own,
        other,
        received,
    )
    result = projected(part, gate, rows_back, x, full_out, out_gain.reshape(1, -1))
    return result.reshape(height, breadth, channels)


def solution(mesh):
    rows, columns = mesh.devices.shape
    split = Mesh(mesh.devices.reshape(rows, columns // 2, 2), ("row", "chip", "core"))
    wide, all_axes = ("chip", "core"), ("row", "chip", "core")
    placed = (
        P("row", wide, None),
        P("row", wide),
        P(),
        P(None, all_axes),
        P(),
        P(),
        P(all_axes, None),
        P(),
        P(),
        P(),
        P(),
        P(all_axes, None),
    )
    return jax.shard_map(
        on_device, mesh=split, in_specs=placed, out_specs=P("row", wide, None), check_vma=False
    )
```

```python
import jax
import jax.numpy as jnp
from jax import lax
from jax.experimental import pallas as pl
from jax.experimental.pallas import tpu as pltpu
from jax.sharding import Mesh, PartitionSpec as P

STATE = 16
HEADS = 32
TILE = 16
CHUNK = 128
LANES = 128
BLOCK = 32
PARTS = CHUNK // BLOCK
STRIDE = 24
LOG2E = 1.4426950408889634
GRANT = 56 * 2**20

f32 = jnp.float32
bf16 = jnp.bfloat16


def dot(a, b, contract=((1,), (0,))):
    return lax.dot_general(a, b, (contract, ((), ())), preferred_element_type=f32)


def shifted(x, axis, step):
    count = lax.axis_size(axis)
    pairs = [(i, i + step) for i in range(count) if 0 <= i + step < count]
    return lax.ppermute(x, axis, pairs)


def diagonal(x, down, right):
    axes = ("row", "chip", "core")
    rows, columns = lax.axis_size("row"), lax.axis_size(("chip", "core"))
    pairs = [
        (r * columns + c, (r + down) * columns + c + right)
        for r in range(rows)
        for c in range(columns)
        if 0 <= r + down < rows and 0 <= c + right < columns
    ]
    return lax.ppermute(x, axes, pairs)


def here():
    return lax.axis_index("row"), 2 * lax.axis_index("chip") + lax.axis_index("core")


def normalized(x, gain):
    average = jnp.mean(x, axis=-1, keepdims=True)
    centered = x - average
    spread = jnp.mean(centered * centered, axis=-1, keepdims=True)
    return centered * lax.rsqrt(spread + 1e-05) * gain


def paired(own_ref, other_ref, core):
    own, other = own_ref[...].astype(f32), other_ref[...].astype(f32)
    return jnp.where(core == 0, own, other), jnp.where(core == 0, other, own)


def rows_of_eight(*pieces):
    count = pieces[0].shape[0] // 8
    parts = [p.reshape(count, 8, p.shape[1]) for p in pieces]
    return jnp.concatenate(parts, axis=1).reshape(-1, pieces[0].shape[1]).astype(bf16)


def input_weights(own_ref, other_ref, core):
    half = own_ref.shape[1] // 2
    even, odd = paired(own_ref, other_ref, core)
    return rows_of_eight(even[:, :half], even[:, half:], odd[:, :half], odd[:, half:])


def parcel_kernel(mask, in_ref, out_ref, proj_ref, parcel_ref):
    place = here()
    row = lax.broadcasted_iota(jnp.int32, (8, LANES), 0)
    lane = lax.broadcasted_iota(jnp.int32, (8, LANES), 1)
    flags = jnp.zeros((8, LANES), f32)
    for i in range(mask.shape[1]):
        flags = jnp.where(
            (row == i) & (lane == place[1]), mask[:, i : i + 1].astype(f32), flags
        )
    turned = in_ref[...].astype(f32)
    parts = [turned[:8], turned[8:], out_ref[...].astype(f32), proj_ref[...].astype(f32), flags]
    at = 0
    for part in parts:
        width = part.shape[1]
        parcel_ref[:, :, at : at + width] = jnp.broadcast_to(
            part.astype(bf16)[None], (parcel_ref.shape[0], 8, width)
        )
        at += width


def parcels(mask, turned, w_out, w_proj, groups):
    width = 2 * turned.shape[1] + w_out.shape[1] + w_proj.shape[1] + LANES
    block = 16
    one = lambda i: (0, 0)
    return pl.pallas_call(
        parcel_kernel,
        grid=(groups // block,),
        in_specs=[
            pl.BlockSpec(mask.shape, one),
            pl.BlockSpec(turned.shape, one),
            pl.BlockSpec(w_out.shape, one),
            pl.BlockSpec(w_proj.shape, one),
        ],
        out_specs=pl.BlockSpec((block, 8, width), lambda i: (i, 0, 0)),
        out_shape=jax.ShapeDtypeStruct((groups, 8, width), bf16),
        compiler_params=pltpu.CompilerParams(vmem_limit_bytes=GRANT),
        name="parcels",
    )(mask, turned, w_out, w_proj)


def head_lanes(ref, first):
    heads = ref.shape[1]
    head = lax.broadcasted_iota(jnp.int32, (heads, LANES), 0)
    lane = lax.broadcasted_iota(jnp.int32, (heads, LANES), 1)
    placed = [
        lax.dot_general(
            ref[...],
            (lane == head + 64 * d).astype(f32),
            (((1,), (0,)), ((), ())),
            precision=lax.Precision.HIGHEST,
            preferred_element_type=f32,
        )
        for d in range(2)
    ]
    return placed[0][first : first + 1] + placed[1][first + 1 : first + 2]


def chunk_terms(values, w_proj, bias, rate, kept):
    coefs = dot(values, w_proj)
    at = lax.broadcasted_iota(jnp.int32, (CHUNK, LANES), 0)
    lane = lax.broadcasted_iota(jnp.int32, (CHUNK, LANES), 1)
    v = coefs + bias
    steps = kept * (jnp.maximum(v, 0.0) + jnp.log1p(jnp.exp(-jnp.abs(v))))
    decays = steps * rate
    lower = ((lane <= at) & (lane // BLOCK == at // BLOCK)).astype(f32).astype(bf16)
    high = decays.astype(bf16)
    rest = decays - high.astype(f32)
    middle = rest.astype(bf16)
    low = (rest - middle.astype(f32)).astype(bf16)
    total = dot(
        jnp.concatenate([lower] * 3, axis=1), jnp.concatenate([high, middle, low], axis=0)
    )
    sums = jnp.where(lane < 64, total, total - decays)
    ends = [total[(b + 1) * BLOCK - 1 : (b + 1) * BLOCK, :] for b in range(PARTS)]
    return coefs, steps, sums, ends


def edge_factors(sums, steps, ends):
    lane = lax.broadcasted_iota(jnp.int32, (CHUNK, LANES), 1)
    end = jnp.concatenate([jnp.broadcast_to(e, (BLOCK, LANES)) for e in ends], axis=0)
    tail = jnp.exp2(jnp.where(lane < 64, sums - end, -sums)) * steps
    enter = jnp.exp2(jnp.where(lane < 64, -sums, sums - end))
    rows = ends + [jnp.zeros((8 - PARTS, LANES), f32)]
    fade = jnp.exp2(-jnp.concatenate(rows, axis=0))
    return tail.astype(bf16), enter.astype(bf16), fade


def head_spread(expand):
    head = lax.broadcasted_iota(jnp.int32, (LANES, expand), 0)
    channel = lax.broadcasted_iota(jnp.int32, (LANES, expand), 1)
    return [(head == channel // 32 + 64 * d).astype(f32).astype(bf16) for d in range(2)]


def by_block(coefs, first):
    lane = lax.broadcasted_iota(jnp.int32, (LANES, PARTS * STATE), 0)
    to = lax.broadcasted_iota(jnp.int32, (LANES, PARTS * STATE), 1)
    copied = dot(coefs, (lane == first + to % STATE).astype(f32).astype(bf16))
    at = lax.broadcasted_iota(jnp.int32, copied.shape, 0)
    place = lax.broadcasted_iota(jnp.int32, copied.shape, 1)
    return jnp.where(at // BLOCK == place // STATE, copied, 0.0).astype(bf16)


def block_states(values, coefs, tail, spread):
    writes, inputs = coefs.astype(bf16), values.astype(f32)
    states = []
    for d in range(2):
        weighted = (inputs * dot(tail, spread[d])).astype(bf16)
        states.append(dot(by_block(writes, 64 * d + 32), weighted, ((0,), (0,))))
    return states


def mixing_scratch():
    return [
        pltpu.VMEM((LANES, CHUNK), f32),
        pltpu.VMEM((LANES, CHUNK), f32),
        pltpu.VMEM((4 * PARTS, 8, LANES), f32),
    ]


def mix_chunk(values, coefs, steps, sums, spread, scratch, more, store):
    sums_t, steps_t, rows = scratch
    expand = values.shape[1]
    sums_t[...], steps_t[...] = sums.T, steps.T
    row_lane = lax.broadcasted_iota(jnp.int32, (8, LANES), 1)
    for a, (ref, first) in enumerate(((sums_t, 0), (sums_t, 64), (steps_t, 0), (steps_t, 64))):
        lines = [ref[pl.ds(first + k, 8, stride=4), :] for k in range(4)]
        for b in range(PARTS):
            merged = None
            for k in range(4):
                turn = (k - b) * BLOCK % LANES
                line = pltpu.roll(lines[k], turn, 1) if turn else lines[k]
                merged = line if merged is None else jnp.where(row_lane // BLOCK == k, line, merged)
            rows[a * PARTS + b] = merged
    at = lax.broadcasted_iota(jnp.int32, (BLOCK, LANES), 0)
    source = lax.broadcasted_iota(jnp.int32, (BLOCK, LANES), 1) % BLOCK
    causal = source <= at
    c = coefs.astype(bf16)
    products = []
    for b in range(PARTS):
        block = c[b * BLOCK : (b + 1) * BLOCK, :]
        four = jnp.concatenate([block] * 4, axis=0)
        forward = dot(block[:, 48:64], four[:, 32:48], ((1,), (1,)))
        backward = dot(block[:, 112:128], four[:, 96:112], ((1,), (1,)))
        products.append(
            (jnp.where(causal, forward, 0.0), jnp.where(source >= at, backward, 0.0))
        )
    high = sums.astype(bf16)
    parts = jnp.concatenate([high, (sums - high.astype(f32)).astype(bf16)], axis=1)
    head_of = lax.broadcasted_iota(jnp.int32, (BLOCK, LANES), 1) // 32
    for pair in range(0, expand, 2 * LANES):
        wide = slice(pair, pair + 2 * LANES)
        own = [
            dot(parts, jnp.concatenate([spread[d][:, wide]] * 2, axis=0)) for d in range(2)
        ]
        extra = more(wide)
        for lane in range(0, 2 * LANES, LANES):
            tile = (pair + lane) // LANES
            lanes = slice(pair + lane, pair + lane + LANES)
            for b in range(PARTS):
                span = slice(b * BLOCK, (b + 1) * BLOCK)
                row = [rows[a * PARTS + b, tile : tile + 1, :] for a in range(4)]
                exponent = jnp.where(
                    causal,
                    row[0] - own[0][span, lane : lane + LANES],
                    own[1][span, lane : lane + LANES] - row[1],
                )
                scale = products[b][0] * row[2] + products[b][1] * row[3]
                mixing = (jnp.exp2(exponent) * scale).astype(bf16)
                inputs = values[span, lanes]
                apart = jnp.concatenate(
                    [jnp.where(head_of == k, inputs, jnp.zeros_like(inputs)) for k in range(4)],
                    axis=0,
                )
                total = dot(mixing, apart)
                if extra is not None:
                    total = total + extra[span, lane : lane + LANES]
                store(span, lanes, total.astype(bf16))


def line_kernel(
    a_ref, own_ref, other_ref, own_flags, other_flags, bias_ref, rate_ref, out_ref, coefs, steps, sums, enters, fades, states, entering, *scratch
):
    place = here()
    length, expand = a_ref.shape
    chunks = length // CHUNK
    part = PARTS * STATE
    lane = lax.broadcasted_iota(jnp.int32, (CHUNK, LANES), 1)
    spread = head_spread(expand)
    w_proj = rows_of_eight(*paired(own_ref, other_ref, place[1] % 2))
    bias, rate = head_lanes(bias_ref, 0), head_lanes(rate_ref, 0) * LOG2E
    flags = own_flags[...].astype(f32) + other_flags[...].astype(f32)
    line = lax.broadcasted_iota(jnp.int32, flags.shape, 0)
    mine = (line // (flags.shape[0] // 4) == place[0]) & (line % 8 == place[1] // TILE)
    mask = jnp.sum(jnp.where(mine, flags, 0.0), axis=0, keepdims=True)
    position = lax.broadcasted_iota(jnp.int32, (CHUNK, LANES), 0)
    for c in range(chunks):
        tile_at = lane == (position + c * CHUNK) // TILE
        kept = jnp.sum(jnp.where(tile_at, mask, 0.0), axis=1, keepdims=True)
        at = slice(c * CHUNK, (c + 1) * CHUNK)
        values = a_ref[at, :]
        k, s, q, ends = chunk_terms(values, w_proj, bias, rate, kept)
        tail, enter, fade = edge_factors(q, s, ends)
        coefs[at, :], steps[at, :], sums[at, :], enters[at, :] = k, s, q, enter
        fades[8 * c : 8 * c + 8, :] = fade
        for d, state in enumerate(block_states(values, k, tail, spread)):
            states[d, c * part : (c + 1) * part, :] = state
    fade = fades[...]
    high = fade.astype(bf16)
    low = (fade - high.astype(f32)).astype(bf16)
    blocks = chunks * PARTS
    for d in range(2):
        decay = dot(high, spread[d]) + dot(low, spread[d])
        running = jnp.zeros((STATE, expand), f32)
        for b in range(blocks) if d == 0 else range(blocks - 1, -1, -1):
            at = slice(b * STATE, (b + 1) * STATE)
            entering[d, at, :] = running.astype(bf16)
            row = b // PARTS * 8 + b % PARTS
            running = running * decay[row : row + 1, :] + states[d, at, :]
    for c in range(chunks):
        at = slice(c * CHUNK, (c + 1) * CHUNK)
        k, enter = coefs[at, :], enters[at, :]
        read = k.astype(bf16)
        reads = [by_block(read, 64 * d + 48) for d in range(2)]

        def carried(lanes):
            total = None
            for d in range(2):
                state = dot(reads[d], entering[d, c * part : (c + 1) * part, lanes])
                term = dot(enter, spread[d][:, lanes]) * state
                total = term if total is None else total + term
            return total

        def store(span, lanes, value):
            out_ref[c * CHUNK + span.start : c * CHUNK + span.stop, lanes] = value

        mix_chunk(
            a_ref[at, :], k, steps[at, :], sums[at, :], spread, scratch, carried, store
        )


def piece_specs(rows, *columns):
    return [pl.BlockSpec((rows, LANES), lambda i, c=c: (0, c)) for c in columns for _ in range(2)]


def swept_lines(values, own, other, bias, rate):
    length, expand = values.shape
    chunks = length // CHUNK
    small = pl.BlockSpec(bias.shape, lambda i: (0, 0))
    return pl.pallas_call(
        line_kernel,
        grid=(1,),
        in_specs=[
            pl.BlockSpec((length, expand), lambda i: (0, 0)),
            *piece_specs(own.shape[0], 12, 14),
            small,
            small,
        ],
        out_specs=pl.BlockSpec((length, expand), lambda i: (0, 0)),
        out_shape=jax.ShapeDtypeStruct((length, expand), bf16),
        scratch_shapes=[
            pltpu.VMEM((length, LANES), f32),
            pltpu.VMEM((length, LANES), f32),
            pltpu.VMEM((length, LANES), f32),
            pltpu.VMEM((length, LANES), bf16),
            pltpu.VMEM((8 * chunks, LANES), f32),
            pltpu.VMEM((2, length // BLOCK * STATE, expand), f32),
            pltpu.VMEM((2, length // BLOCK * STATE, expand), bf16),
            *mixing_scratch(),
        ],
        compiler_params=pltpu.CompilerParams(vmem_limit_bytes=GRANT),
        cost_estimate=pl.CostEstimate(
            flops=6 * 2**30, bytes_accessed=3 * 2**20, transcendentals=2**21
        ),
        name="sweep_rows",
    )(values, own, other, own, other, bias, rate)


def column_states(
    values_ref, own_ref, other_ref, own_flags, other_flags, bias_ref, rate_ref, coefs_ref, steps_ref, sums_ref, read_ref, slot_refs
):
    row, column = here()
    expand = values_ref.shape[1]
    slots = len(slot_refs)
    states = slot_refs[0].shape[0] - 16
    groups = values_ref.shape[0] // CHUNK
    part = states // groups
    lane = lax.broadcasted_iota(jnp.int32, (CHUNK, LANES), 1)
    flags = (own_flags[...].astype(f32) + other_flags[...].astype(f32)).astype(bf16)
    to = lax.broadcasted_iota(jnp.int32, (CHUNK, flags.shape[0]), 0)
    source = lax.broadcasted_iota(jnp.int32, (CHUNK, flags.shape[0]), 1)
    mine = (source // (flags.shape[0] // (slots + 1)) == row) & (
        source % 8 == to % BLOCK // TILE
    )
    marks = dot(mine.astype(f32).astype(bf16), flags)
    kept = jnp.sum(jnp.where(lane == column, marks, 0.0), axis=1, keepdims=True)
    proj = rows_of_eight(*paired(own_ref, other_ref, column % 2))
    bias, rate = head_lanes(bias_ref, 2), head_lanes(rate_ref, 2) * LOG2E
    spread = head_spread(expand)
    rows = [[] for _ in slot_refs]
    for g in range(groups):
        at = slice(g * CHUNK, (g + 1) * CHUNK)
        values = values_ref[at, :]
        k, s, q, ends = chunk_terms(values, proj, bias, rate, kept)
        coefs_ref[at, :], steps_ref[at, :], sums_ref[at, :] = k.astype(bf16), s.astype(bf16), q
        tail, enter, fade = edge_factors(q, s, ends)
        read_ref[at, :] = jnp.where(lane % 64 >= 48, k.astype(bf16), enter)
        high = fade.astype(bf16)
        low = (fade - high.astype(f32)).astype(bf16)
        down, up = block_states(values, k, tail, spread)
        fades = [dot(high, m) + dot(low, m) for m in spread]
        for d, ref in enumerate(slot_refs):
            onward = row + d + 1 <= slots
            ref[g * part : (g + 1) * part, :] = jnp.where(onward, down, up).astype(bf16)
            rows[d].append(jnp.where(onward, fades[0], fades[1])[:PARTS])
    for d, ref in enumerate(slot_refs):
        ref[states:, :] = jnp.concatenate(rows[d], axis=0).astype(bf16)


def filter_kernel(
    x_ref, gain_ref, own_ref, other_ref, taps_ref, bias_ref, *refs
):
    place = here()
    column_refs, (act_ref, turned_ref), refs = refs[:6], refs[6:8], refs[8:]
    outs, slot_refs, (normed, branch, order, turned) = refs[:4], refs[4:-4], refs[-4:]
    padded = x_ref.shape[0]
    tokens, width = act_ref.shape
    height = padded // STRIDE - 2
    breadth = tokens // height

    @pl.when(pl.program_id(0) == 0)
    def _():
        step = 64
        for at in range(0, padded, step):
            x = x_ref[at : at + step, :].astype(f32)
            normed[at : at + step, :] = normalized(x, gain_ref[...]).astype(bf16)
        to = lax.broadcasted_iota(jnp.int32, (tokens, tokens), 0)
        source = lax.broadcasted_iota(jnp.int32, (tokens, tokens), 1)
        w, h = to // height, to % height
        order[...] = (source == h * breadth + w).astype(f32).astype(bf16)

    weights = input_weights(own_ref, other_ref, place[1] % 2)
    product = dot(normed[...], weights, ((1,), (1,)))
    branch[...] = product.astype(bf16).astype(f32)
    rows = 4
    span = rows * STRIDE + 8
    for lane in range(0, width, LANES):
        lanes = slice(lane, lane + LANES)
        taps = [taps_ref[k : k + 1, lanes] for k in range(9)]
        for h in range(0, height, rows):
            windows = [
                branch[(h + i) * STRIDE : (h + i) * STRIDE + span, lanes] for i in range(3)
            ]
            left, middle, right = [
                windows[0] * taps[j] + windows[1] * taps[3 + j] + windows[2] * taps[6 + j]
                for j in range(3)
            ]
            convolved = (
                middle
                + pltpu.roll(left, 1, 0)
                + pltpu.roll(right, span - 1, 0)
                + bias_ref[:, lanes]
            )
            activated = convolved / (1.0 + jnp.exp(-convolved))
            kept = activated[: rows * STRIDE].reshape(rows, STRIDE, LANES)[:, 8:, :]
            act_ref[h * breadth : (h + rows) * breadth, lanes] = kept.reshape(
                rows * breadth, LANES
            ).astype(bf16)
    across = dot(order[...], act_ref[...]).astype(bf16)
    turned_ref[...] = across
    step = pl.program_id(0)
    turned[:, pl.ds(pl.multiple_of(step * width, width), width)] = across

    @pl.when(step == pl.num_programs(0) - 1)
    def _():
        column_states(turned, *column_refs, *outs, slot_refs)


def filtered(x, gain, own, other, taps, bias, tokens, dt_bias, rate, slots):
    expand = bias.shape[1]
    padded, channels = x.shape
    width = 256
    states = tokens // BLOCK * STATE + 16
    one = lambda c: (0, 0)
    piece = pl.BlockSpec((width // 4, 2 * channels), lambda c: (c, 0))
    return pl.pallas_call(
        filter_kernel,
        grid=(expand // width,),
        in_specs=[
            pl.BlockSpec((padded, channels), lambda c: (0, 0)),
            pl.BlockSpec((1, channels), lambda c: (0, 0)),
            piece,
            piece,
            pl.BlockSpec((9, width), lambda c: (0, c)),
            pl.BlockSpec((1, width), lambda c: (0, c)),
            *piece_specs(own.shape[0], 13, 14),
            pl.BlockSpec(dt_bias.shape, one),
            pl.BlockSpec(rate.shape, one),
        ],
        out_specs=[pl.BlockSpec((tokens, width), lambda c: (0, c))] * 2
        + [pl.BlockSpec((tokens, LANES), one)] * 4
        + [pl.BlockSpec((states, expand), one)] * (slots - 1),
        out_shape=[jax.ShapeDtypeStruct((tokens, expand), bf16)] * 2
        + [jax.ShapeDtypeStruct((tokens, LANES), t) for t in (bf16, bf16, f32, bf16)]
        + [jax.ShapeDtypeStruct((states, expand), bf16)] * (slots - 1),
        scratch_shapes=[
            pltpu.VMEM((padded, channels), bf16),
            pltpu.VMEM((padded, width), f32),
            pltpu.VMEM((tokens, tokens), bf16),
            pltpu.VMEM((tokens, expand), bf16),
        ],
        compiler_params=pltpu.CompilerParams(vmem_limit_bytes=GRANT),
        cost_estimate=pl.CostEstimate(
            flops=2 * padded * channels * expand, bytes_accessed=6 * 2**20, transcendentals=tokens * expand
        ),
        name="norm_project_filter",
    )(x, gain, own, other, taps, bias, own, other, own, other, dt_bias, rate)


def mix_kernel(a_ref, coefs_ref, steps_ref, sums_ref, out_ref, spread, *scratch):
    @pl.when(pl.program_id(0) == 0)
    def _():
        for d, matrix in enumerate(head_spread(a_ref.shape[1])):
            spread[d] = matrix

    def store(span, lanes, value):
        out_ref[span, lanes] = value

    mix_chunk(
        a_ref[...],
        coefs_ref[...],
        steps_ref[...].astype(f32),
        sums_ref[...],
        [spread[0], spread[1]],
        scratch,
        lambda lanes: None,
        store,
    )


def mixed_columns(values, coefs, steps, sums):
    tokens, expand = values.shape
    block = pl.BlockSpec((CHUNK, expand), lambda i: (i, 0))
    thin = pl.BlockSpec((CHUNK, LANES), lambda i: (i, 0))
    return pl.pallas_call(
        mix_kernel,
        grid=(tokens // CHUNK,),
        in_specs=[block, thin, thin, thin],
        out_specs=block,
        out_shape=jax.ShapeDtypeStruct((tokens, expand), bf16),
        scratch_shapes=[pltpu.VMEM((2, LANES, expand), bf16), *mixing_scratch()],
        compiler_params=pltpu.CompilerParams(vmem_limit_bytes=GRANT),
        cost_estimate=pl.CostEstimate(
            flops=2**32, bytes_accessed=3 * 2**20, transcendentals=2**21
        ),
        name="mix_columns",
    )(values, coefs, steps, sums)


def entering_kernel(
    local_ref, read_ref, act_ref, skip_ref, x_ref, gain_ref, own_gate, other_gate, own_out, other_out, *refs
):
    place = here()
    slots = len(refs) - 5
    slot_refs, (part_ref, gate_ref, w_out_ref, w_gate, columns) = refs[:slots], refs[slots:]
    expand = local_ref.shape[1]
    states = slot_refs[0].shape[0] - 16
    groups = local_ref.shape[0] // CHUNK
    part = states // groups
    lines = part // STATE
    height = CHUNK // lines
    spread = head_spread(expand)
    row = place[0]
    decays = [ref[states:, :].astype(f32) for ref in slot_refs]
    for g in range(groups):
        at = slice(g * CHUNK, (g + 1) * CHUNK)
        total = local_ref[at, :].astype(f32)
        read = read_ref[at, :]
        for d in range(2):
            order = range(slots) if d == 0 else range(slots - 1, -1, -1)
            entering, product = [], [None] * lines
            sums = [jnp.zeros((STATE, expand), f32)] * lines
            for step, k in enumerate(order):
                reaches = row > step if d == 0 else row + step + 1 <= slots
                for line in range(lines):
                    at_state = g * part + line * STATE
                    state = slot_refs[k][at_state : at_state + STATE, :].astype(f32)
                    if product[line] is not None:
                        state = state * product[line]
                    sums[line] = sums[line] + jnp.where(reaches, state, 0.0)
                    fade = decays[k][g * lines + line : g * lines + line + 1, :]
                    product[line] = fade if product[line] is None else product[line] * fade
            entering = jnp.concatenate(sums, axis=0).astype(bf16)
            carried = dot(by_block(read, 64 * d + 48), entering)
            total = total + dot(read, spread[d]) * carried
        columns[at, :] = total.astype(bf16)
    w_gate[...] = input_weights(own_gate, other_gate, place[1] % 2)
    w_out_ref[...] = rows_of_eight(*paired(own_out, other_out, place[1] % 2))
    tokens = local_ref.shape[0]
    breadth = tokens // height
    for g in range(groups):
        at = slice(g * CHUNK, (g + 1) * CHUNK)
        to = lax.broadcasted_iota(jnp.int32, (CHUNK, tokens), 0) + g * CHUNK
        source = lax.broadcasted_iota(jnp.int32, (CHUNK, tokens), 1)
        w, h = source // height, source % height
        back = (to == h * breadth + w).astype(f32).astype(bf16)
        direct = skip_ref[...] * act_ref[at, :].astype(f32)
        part_ref[at, :] = dot(back, columns[...]) + direct
        normed = normalized(x_ref[at, :].astype(f32), gain_ref[...]).astype(bf16)
        gating = dot(normed, w_gate[...], ((1,), (1,))).astype(bf16).astype(f32)
        gate_ref[at, :] = (gating / (1.0 + jnp.exp(-gating))).astype(bf16)


def entered(local, read, act, skip, x, gain, own, other, slots):
    tokens, expand = local.shape
    pairs, channels = own.shape[0], x.shape[1]
    whole = lambda x: pl.BlockSpec(x.shape, lambda i: (0, 0))
    gate = pl.BlockSpec((pairs // 2, 2 * channels), lambda i: (1, 0))
    last = pl.BlockSpec((pairs, channels), lambda i: (0, 2))
    shapes = [
        jax.ShapeDtypeStruct((tokens, expand), f32),
        jax.ShapeDtypeStruct((tokens, expand), bf16),
        jax.ShapeDtypeStruct((expand, channels), bf16),
    ]
    return pl.pallas_call(
        entering_kernel,
        grid=(1,),
        in_specs=[whole(a) for a in (local, read, act, skip, x, gain)]
        + [gate, gate, last, last]
        + [whole(a) for a in slots],
        out_specs=[whole(a) for a in shapes],
        out_shape=shapes,
        scratch_shapes=[
            pltpu.VMEM((expand, channels), bf16),
            pltpu.VMEM((tokens, expand), bf16),
        ],
        compiler_params=pltpu.CompilerParams(vmem_limit_bytes=GRANT),
        cost_estimate=pl.CostEstimate(
            flops=2**32, bytes_accessed=12 * 2**20, transcendentals=2**19
        ),
        name="enter_columns",
    )(local, read, act, skip, x, gain, own, other, own, other, *slots)


def output_kernel(part_ref, gate_ref, rows_ref, x_ref, w_ref, out_gain_ref, out_ref):
    summed = part_ref[...] + rows_ref[...].astype(f32)
    mixed = (normalized(summed, out_gain_ref[...]) * gate_ref[...].astype(f32)).astype(bf16)
    out_ref[...] = (x_ref[...].astype(f32) + dot(mixed, w_ref[...])).astype(bf16)


def projected(part, gate, rows, x, w_out, out_gain):
    tokens, expand = part.shape
    channels = x.shape[1]
    block = 128
    one = lambda i: (0, 0)
    wide = pl.BlockSpec((block, expand), lambda i: (i, 0))
    narrow = pl.BlockSpec((block, channels), lambda i: (i, 0))
    return pl.pallas_call(
        output_kernel,
        grid=(tokens // block,),
        in_specs=[
            wide,
            wide,
            wide,
            narrow,
            pl.BlockSpec((expand, channels), one),
            pl.BlockSpec((1, expand), one),
        ],
        out_specs=narrow,
        out_shape=jax.ShapeDtypeStruct((tokens, channels), bf16),
        compiler_params=pltpu.CompilerParams(vmem_limit_bytes=GRANT),
        name="gate_and_project",
    )(part, gate, rows, x, w_out, out_gain)


def on_device(
    tokens, tile_mask, norm_gain, w_in, conv_weight, conv_bias, w_proj, dt_bias, decay_rate, skip_gain, out_gain, w_out
):
    wide = ("chip", "core")
    count_row, count_chip = lax.axis_size("row"), lax.axis_size("chip")
    height, breadth, channels = tokens.shape
    local = height * breadth
    expand = conv_bias.shape[0]

    groups = count_row * count_chip
    parcel = parcels(tile_mask.T, w_in.T, w_out, w_proj, groups)
    own = lax.all_to_all(parcel, ("row", "chip"), 0, 0, tiled=True)
    above, below = shifted(tokens[-1:], "row", 1), shifted(tokens[:1], "row", -1)
    tall = jnp.concatenate([above, tokens, below], axis=0)
    before, after = [
        jnp.concatenate(
            [
                diagonal(tokens[-1:, edge], 1, step),
                shifted(tokens[:, edge], wide, step),
                diagonal(tokens[:1, edge], -1, step),
            ],
            axis=0,
        )
        for edge, step in ((slice(breadth - 1, breadth), 1), (slice(0, 1), -1))
    ]
    after_last = jnp.concatenate([jnp.zeros_like(after[:1]), after], axis=0)
    body = jnp.concatenate(
        [after_last[:-1], jnp.zeros((height + 2, 6, channels), bf16), before, tall], axis=1
    ).reshape((height + 2) * STRIDE, channels)
    x_ext = jnp.concatenate([body, after_last[-1], jnp.zeros((15, channels), bf16)], axis=0)

    own, x_ext = lax.optimization_barrier((own, x_ext))
    other = lax.ppermute(own, "core", [(0, 1), (1, 0)])
    own, other = [p.reshape(groups * 8, p.shape[2]) for p in (own, other)]

    act, turned, coefs, steps, sums, read, *states = filtered(
        x_ext,
        norm_gain.reshape(1, -1),
        own,
        other,
        conv_weight,
        conv_bias.reshape(1, -1),
        local,
        dt_bias,
        decay_rate,
        count_row,
    )
    def spun(piece, d):
        return lax.ppermute(piece, "row", [(i, (i + d) % count_row) for i in range(count_row)])

    def dealt(x):
        return lax.all_to_all(
            x.reshape(-1, breadth, expand), wide, 0, 0, tiled=True
        ).reshape(-1, expand)

    lines = dealt(act)
    received = [spun(piece, d + 1) for d, piece in enumerate(states)]
    columns_local = mixed_columns(turned, coefs, steps, sums)
    lines, columns_local = lax.optimization_barrier((lines, columns_local))
    rows_out = swept_lines(lines, own, other, dt_bias, decay_rate)
    rows_out, received = lax.optimization_barrier((rows_out, received))
    rows_back = dealt(rows_out)
    x = tokens.reshape(local, channels)
    part, gate, full_out = entered(
        columns_local,
        read,
        act,
        skip_gain.reshape(1, -1),
        x,
        norm_gain.reshape(1, -1),
        own,
        other,
        received,
    )
    result = projected(part, gate, rows_back, x, full_out, out_gain.reshape(1, -1))
    return result.reshape(height, breadth, channels)


def solution(mesh):
    rows, columns = mesh.devices.shape
    split = Mesh(mesh.devices.reshape(rows, columns // 2, 2), ("row", "chip", "core"))
    wide, all_axes = ("chip", "core"), ("row", "chip", "core")
    placed = (
        P("row", wide, None),
        P("row", wide),
        P(),
        P(None, all_axes),
        P(),
        P(),
        P(all_axes, None),
        P(),
        P(),
        P(),
        P(),
        P(all_axes, None),
    )
    return jax.shard_map(
        on_device, mesh=split, in_specs=placed, out_specs=P("row", wide, None), check_vma=False
    )
```

```python
import jax
import jax.numpy as jnp
from jax import lax
from jax.experimental import pallas as pl
from jax.experimental.pallas import tpu as pltpu
from jax.sharding import Mesh, PartitionSpec as P

STATE = 16
HEADS = 32
TILE = 16
CHUNK = 128
LANES = 128
BLOCK = 32
PARTS = CHUNK // BLOCK
STRIDE = 24
LOG2E = 1.4426950408889634
GRANT = 56 * 2**20

f32 = jnp.float32
bf16 = jnp.bfloat16


def dot(a, b, contract=((1,), (0,))):
    return lax.dot_general(a, b, (contract, ((), ())), preferred_element_type=f32)


def shifted(x, axis, step):
    count = lax.axis_size(axis)
    pairs = [(i, i + step) for i in range(count) if 0 <= i + step < count]
    return lax.ppermute(x, axis, pairs)


def diagonal(x, down, right):
    axes = ("row", "chip", "core")
    rows, columns = lax.axis_size("row"), lax.axis_size(("chip", "core"))
    pairs = [
        (r * columns + c, (r + down) * columns + c + right)
        for r in range(rows)
        for c in range(columns)
        if 0 <= r + down < rows and 0 <= c + right < columns
    ]
    return lax.ppermute(x, axes, pairs)


def here():
    return lax.axis_index("row"), 2 * lax.axis_index("chip") + lax.axis_index("core")


def normalized(x, gain):
    average = jnp.mean(x, axis=-1, keepdims=True)
    centered = x - average
    spread = jnp.mean(centered * centered, axis=-1, keepdims=True)
    return centered * lax.rsqrt(spread + 1e-05) * gain


def paired(own_ref, other_ref, core):
    own, other = own_ref[...].astype(f32), other_ref[...].astype(f32)
    return jnp.where(core == 0, own, other), jnp.where(core == 0, other, own)


def rows_of_eight(*pieces):
    count = pieces[0].shape[0] // 8
    parts = [p.reshape(count, 8, p.shape[1]) for p in pieces]
    return jnp.concatenate(parts, axis=1).reshape(-1, pieces[0].shape[1]).astype(bf16)


def input_weights(own_ref, other_ref, core):
    half = own_ref.shape[1] // 2
    even, odd = paired(own_ref, other_ref, core)
    return rows_of_eight(even[:, :half], even[:, half:], odd[:, :half], odd[:, half:])


def parcel_kernel(mask, in_ref, out_ref, proj_ref, parcel_ref):
    place = here()
    row = lax.broadcasted_iota(jnp.int32, (8, LANES), 0)
    lane = lax.broadcasted_iota(jnp.int32, (8, LANES), 1)
    flags = jnp.zeros((8, LANES), f32)
    for i in range(mask.shape[1]):
        flags = jnp.where(
            (row == i) & (lane == place[1]), mask[:, i : i + 1].astype(f32), flags
        )
    turned = in_ref[...].astype(f32)
    parts = [turned[:8], turned[8:], out_ref[...].astype(f32), proj_ref[...].astype(f32), flags]
    at = 0
    for part in parts:
        width = part.shape[1]
        parcel_ref[:, :, at : at + width] = jnp.broadcast_to(
            part.astype(bf16)[None], (parcel_ref.shape[0], 8, width)
        )
        at += width


def parcels(mask, turned, w_out, w_proj, groups):
    width = 2 * turned.shape[1] + w_out.shape[1] + w_proj.shape[1] + LANES
    block = 32
    one = lambda i: (0, 0)
    return pl.pallas_call(
        parcel_kernel,
        grid=(groups // block,),
        in_specs=[
            pl.BlockSpec(mask.shape, one),
            pl.BlockSpec(turned.shape, one),
            pl.BlockSpec(w_out.shape, one),
            pl.BlockSpec(w_proj.shape, one),
        ],
        out_specs=pl.BlockSpec((block, 8, width), lambda i: (i, 0, 0)),
        out_shape=jax.ShapeDtypeStruct((groups, 8, width), bf16),
        compiler_params=pltpu.CompilerParams(vmem_limit_bytes=GRANT),
        name="parcels",
    )(mask, turned, w_out, w_proj)


def head_lanes(ref, first):
    heads = ref.shape[1]
    head = lax.broadcasted_iota(jnp.int32, (heads, LANES), 0)
    lane = lax.broadcasted_iota(jnp.int32, (heads, LANES), 1)
    placed = [
        lax.dot_general(
            ref[...],
            (lane == head + 64 * d).astype(f32),
            (((1,), (0,)), ((), ())),
            precision=lax.Precision.HIGHEST,
            preferred_element_type=f32,
        )
        for d in range(2)
    ]
    return placed[0][first : first + 1] + placed[1][first + 1 : first + 2]


def chunk_terms(values, w_proj, bias, rate, kept):
    coefs = dot(values, w_proj)
    at = lax.broadcasted_iota(jnp.int32, (CHUNK, LANES), 0)
    lane = lax.broadcasted_iota(jnp.int32, (CHUNK, LANES), 1)
    v = coefs + bias
    steps = kept * (jnp.maximum(v, 0.0) + jnp.log1p(jnp.exp(-jnp.abs(v))))
    decays = steps * rate
    lower = ((lane <= at) & (lane // BLOCK == at // BLOCK)).astype(f32).astype(bf16)
    high = decays.astype(bf16)
    rest = decays - high.astype(f32)
    middle = rest.astype(bf16)
    low = (rest - middle.astype(f32)).astype(bf16)
    total = dot(
        jnp.concatenate([lower] * 3, axis=1), jnp.concatenate([high, middle, low], axis=0)
    )
    sums = jnp.where(lane < 64, total, total - decays)
    ends = [total[(b + 1) * BLOCK - 1 : (b + 1) * BLOCK, :] for b in range(PARTS)]
    return coefs, steps, sums, ends


def edge_factors(sums, steps, ends):
    lane = lax.broadcasted_iota(jnp.int32, (CHUNK, LANES), 1)
    end = jnp.concatenate([jnp.broadcast_to(e, (BLOCK, LANES)) for e in ends], axis=0)
    tail = jnp.exp2(jnp.where(lane < 64, sums - end, -sums)) * steps
    enter = jnp.exp2(jnp.where(lane < 64, -sums, sums - end))
    rows = ends + [jnp.zeros((8 - PARTS, LANES), f32)]
    fade = jnp.exp2(-jnp.concatenate(rows, axis=0))
    return tail.astype(bf16), enter.astype(bf16), fade


def head_spread(expand):
    head = lax.broadcasted_iota(jnp.int32, (LANES, expand), 0)
    channel = lax.broadcasted_iota(jnp.int32, (LANES, expand), 1)
    return [(head == channel // 32 + 64 * d).astype(f32).astype(bf16) for d in range(2)]


def by_block(coefs, first):
    lane = lax.broadcasted_iota(jnp.int32, (LANES, PARTS * STATE), 0)
    to = lax.broadcasted_iota(jnp.int32, (LANES, PARTS * STATE), 1)
    copied = dot(coefs, (lane == first + to % STATE).astype(f32).astype(bf16))
    at = lax.broadcasted_iota(jnp.int32, copied.shape, 0)
    place = lax.broadcasted_iota(jnp.int32, copied.shape, 1)
    return jnp.where(at // BLOCK == place // STATE, copied, 0.0).astype(bf16)


def block_states(values, coefs, tail, spread):
    writes, inputs = coefs.astype(bf16), values.astype(f32)
    states = []
    for d in range(2):
        weighted = (inputs * dot(tail, spread[d])).astype(bf16)
        states.append(dot(by_block(writes, 64 * d + 32), weighted, ((0,), (0,))))
    return states


def mixing_scratch():
    return [
        pltpu.VMEM((LANES, CHUNK), f32),
        pltpu.VMEM((LANES, CHUNK), f32),
        pltpu.VMEM((4 * PARTS, 8, LANES), f32),
    ]


def mix_chunk(values, coefs, steps, sums, spread, scratch, more, store):
    sums_t, steps_t, rows = scratch
    expand = values.shape[1]
    sums_t[...], steps_t[...] = sums.T, steps.T
    row_lane = lax.broadcasted_iota(jnp.int32, (8, LANES), 1)
    for a, (ref, first) in enumerate(((sums_t, 0), (sums_t, 64), (steps_t, 0), (steps_t, 64))):
        lines = [ref[pl.ds(first + k, 8, stride=4), :] for k in range(4)]
        for b in range(PARTS):
            merged = None
            for k in range(4):
                turn = (k - b) * BLOCK % LANES
                line = pltpu.roll(lines[k], turn, 1) if turn else lines[k]
                merged = line if merged is None else jnp.where(row_lane // BLOCK == k, line, merged)
            rows[a * PARTS + b] = merged
    at = lax.broadcasted_iota(jnp.int32, (BLOCK, LANES), 0)
    source = lax.broadcasted_iota(jnp.int32, (BLOCK, LANES), 1) % BLOCK
    causal = source <= at
    c = coefs.astype(bf16)
    products = []
    for b in range(PARTS):
        block = c[b * BLOCK : (b + 1) * BLOCK, :]
        four = jnp.concatenate([block] * 4, axis=0)
        forward = dot(block[:, 48:64], four[:, 32:48], ((1,), (1,)))
        backward = dot(block[:, 112:128], four[:, 96:112], ((1,), (1,)))
        products.append(
            (jnp.where(causal, forward, 0.0), jnp.where(source >= at, backward, 0.0))
        )
    high = sums.astype(bf16)
    parts = jnp.concatenate([high, (sums - high.astype(f32)).astype(bf16)], axis=1)
    head_of = lax.broadcasted_iota(jnp.int32, (BLOCK, LANES), 1) // 32
    for pair in range(0, expand, 2 * LANES):
        wide = slice(pair, pair + 2 * LANES)
        own = [
            dot(parts, jnp.concatenate([spread[d][:, wide]] * 2, axis=0)) for d in range(2)
        ]
        extra = more(wide)
        for lane in range(0, 2 * LANES, LANES):
            tile = (pair + lane) // LANES
            lanes = slice(pair + lane, pair + lane + LANES)
            for b in range(PARTS):
                span = slice(b * BLOCK, (b + 1) * BLOCK)
                row = [rows[a * PARTS + b, tile : tile + 1, :] for a in range(4)]
                exponent = jnp.where(
                    causal,
                    row[0] - own[0][span, lane : lane + LANES],
                    own[1][span, lane : lane + LANES] - row[1],
                )
                scale = products[b][0] * row[2] + products[b][1] * row[3]
                mixing = (jnp.exp2(exponent) * scale).astype(bf16)
                inputs = values[span, lanes]
                apart = jnp.concatenate(
                    [jnp.where(head_of == k, inputs, jnp.zeros_like(inputs)) for k in range(4)],
                    axis=0,
                )
                total = dot(mixing, apart)
                if extra is not None:
                    total = total + extra[span, lane : lane + LANES]
                store(span, lanes, total.astype(bf16))


def line_kernel(
    a_ref, own_ref, other_ref, own_flags, other_flags, bias_ref, rate_ref, out_ref, coefs, steps, sums, enters, fades, states, entering, *scratch
):
    place = here()
    length, expand = a_ref.shape
    chunks = length // CHUNK
    part = PARTS * STATE
    lane = lax.broadcasted_iota(jnp.int32, (CHUNK, LANES), 1)
    spread = head_spread(expand)
    w_proj = rows_of_eight(*paired(own_ref, other_ref, place[1] % 2))
    bias, rate = head_lanes(bias_ref, 0), head_lanes(rate_ref, 0) * LOG2E
    flags = own_flags[...].astype(f32) + other_flags[...].astype(f32)
    line = lax.broadcasted_iota(jnp.int32, flags.shape, 0)
    mine = (line // (flags.shape[0] // 4) == place[0]) & (line % 8 == place[1] // TILE)
    mask = jnp.sum(jnp.where(mine, flags, 0.0), axis=0, keepdims=True)
    position = lax.broadcasted_iota(jnp.int32, (CHUNK, LANES), 0)
    for c in range(chunks):
        tile_at = lane == (position + c * CHUNK) // TILE
        kept = jnp.sum(jnp.where(tile_at, mask, 0.0), axis=1, keepdims=True)
        at = slice(c * CHUNK, (c + 1) * CHUNK)
        values = a_ref[at, :]
        k, s, q, ends = chunk_terms(values, w_proj, bias, rate, kept)
        tail, enter, fade = edge_factors(q, s, ends)
        coefs[at, :], steps[at, :], sums[at, :], enters[at, :] = k, s, q, enter
        fades[8 * c : 8 * c + 8, :] = fade
        for d, state in enumerate(block_states(values, k, tail, spread)):
            states[d, c * part : (c + 1) * part, :] = state
    fade = fades[...]
    high = fade.astype(bf16)
    low = (fade - high.astype(f32)).astype(bf16)
    blocks = chunks * PARTS
    for d in range(2):
        decay = dot(high, spread[d]) + dot(low, spread[d])
        running = jnp.zeros((STATE, expand), f32)
        for b in range(blocks) if d == 0 else range(blocks - 1, -1, -1):
            at = slice(b * STATE, (b + 1) * STATE)
            entering[d, at, :] = running.astype(bf16)
            row = b // PARTS * 8 + b % PARTS
            running = running * decay[row : row + 1, :] + states[d, at, :]
    for c in range(chunks):
        at = slice(c * CHUNK, (c + 1) * CHUNK)
        k, enter = coefs[at, :], enters[at, :]
        read = k.astype(bf16)
        reads = [by_block(read, 64 * d + 48) for d in range(2)]

        def carried(lanes):
            total = None
            for d in range(2):
                state = dot(reads[d], entering[d, c * part : (c + 1) * part, lanes])
                term = dot(enter, spread[d][:, lanes]) * state
                total = term if total is None else total + term
            return total

        def store(span, lanes, value):
            out_ref[c * CHUNK + span.start : c * CHUNK + span.stop, lanes] = value

        mix_chunk(
            a_ref[at, :], k, steps[at, :], sums[at, :], spread, scratch, carried, store
        )


def piece_specs(rows, *columns):
    return [pl.BlockSpec((rows, LANES), lambda i, c=c: (0, c)) for c in columns for _ in range(2)]


def swept_lines(values, own, other, bias, rate):
    length, expand = values.shape
    chunks = length // CHUNK
    small = pl.BlockSpec(bias.shape, lambda i: (0, 0))
    return pl.pallas_call(
        line_kernel,
        grid=(1,),
        in_specs=[
            pl.BlockSpec((length, expand), lambda i: (0, 0)),
            *piece_specs(own.shape[0], 12, 14),
            small,
            small,
        ],
        out_specs=pl.BlockSpec((length, expand), lambda i: (0, 0)),
        out_shape=jax.ShapeDtypeStruct((length, expand), bf16),
        scratch_shapes=[
            pltpu.VMEM((length, LANES), f32),
            pltpu.VMEM((length, LANES), f32),
            pltpu.VMEM((length, LANES), f32),
            pltpu.VMEM((length, LANES), bf16),
            pltpu.VMEM((8 * chunks, LANES), f32),
            pltpu.VMEM((2, length // BLOCK * STATE, expand), f32),
            pltpu.VMEM((2, length // BLOCK * STATE, expand), bf16),
            *mixing_scratch(),
        ],
        compiler_params=pltpu.CompilerParams(vmem_limit_bytes=GRANT),
        cost_estimate=pl.CostEstimate(
            flops=6 * 2**30, bytes_accessed=3 * 2**20, transcendentals=2**21
        ),
        name="sweep_rows",
    )(values, own, other, own, other, bias, rate)


def column_states(
    values_ref, own_ref, other_ref, own_flags, other_flags, bias_ref, rate_ref, coefs_ref, steps_ref, sums_ref, read_ref, slot_refs
):
    row, column = here()
    expand = values_ref.shape[1]
    slots = len(slot_refs)
    states = slot_refs[0].shape[0] - 16
    groups = values_ref.shape[0] // CHUNK
    part = states // groups
    lane = lax.broadcasted_iota(jnp.int32, (CHUNK, LANES), 1)
    flags = (own_flags[...].astype(f32) + other_flags[...].astype(f32)).astype(bf16)
    to = lax.broadcasted_iota(jnp.int32, (CHUNK, flags.shape[0]), 0)
    source = lax.broadcasted_iota(jnp.int32, (CHUNK, flags.shape[0]), 1)
    mine = (source // (flags.shape[0] // (slots + 1)) == row) & (
        source % 8 == to % BLOCK // TILE
    )
    marks = dot(mine.astype(f32).astype(bf16), flags)
    kept = jnp.sum(jnp.where(lane == column, marks, 0.0), axis=1, keepdims=True)
    proj = rows_of_eight(*paired(own_ref, other_ref, column % 2))
    bias, rate = head_lanes(bias_ref, 2), head_lanes(rate_ref, 2) * LOG2E
    spread = head_spread(expand)
    rows = [[] for _ in slot_refs]
    for g in range(groups):
        at = slice(g * CHUNK, (g + 1) * CHUNK)
        values = values_ref[at, :]
        k, s, q, ends = chunk_terms(values, proj, bias, rate, kept)
        coefs_ref[at, :], steps_ref[at, :], sums_ref[at, :] = k.astype(bf16), s.astype(bf16), q
        tail, enter, fade = edge_factors(q, s, ends)
        read_ref[at, :] = jnp.where(lane % 64 >= 48, k.astype(bf16), enter)
        high = fade.astype(bf16)
        low = (fade - high.astype(f32)).astype(bf16)
        down, up = block_states(values, k, tail, spread)
        fades = [dot(high, m) + dot(low, m) for m in spread]
        for d, ref in enumerate(slot_refs):
            onward = row + d + 1 <= slots
            ref[g * part : (g + 1) * part, :] = jnp.where(onward, down, up).astype(bf16)
            rows[d].append(jnp.where(onward, fades[0], fades[1])[:PARTS])
    for d, ref in enumerate(slot_refs):
        ref[states:, :] = jnp.concatenate(rows[d], axis=0).astype(bf16)


def filter_kernel(
    x_ref, gain_ref, own_ref, other_ref, taps_ref, bias_ref, *refs
):
    place = here()
    column_refs, (act_ref, turned_ref), refs = refs[:6], refs[6:8], refs[8:]
    outs, slot_refs, (normed, branch, order, turned) = refs[:4], refs[4:-4], refs[-4:]
    padded = x_ref.shape[0]
    tokens, width = act_ref.shape
    height = padded // STRIDE - 2
    breadth = tokens // height

    @pl.when(pl.program_id(0) == 0)
    def _():
        step = 64
        for at in range(0, padded, step):
            x = x_ref[at : at + step, :].astype(f32)
            normed[at : at + step, :] = normalized(x, gain_ref[...]).astype(bf16)
        to = lax.broadcasted_iota(jnp.int32, (tokens, tokens), 0)
        source = lax.broadcasted_iota(jnp.int32, (tokens, tokens), 1)
        w, h = to // height, to % height
        order[...] = (source == h * breadth + w).astype(f32).astype(bf16)

    weights = input_weights(own_ref, other_ref, place[1] % 2)
    product = dot(normed[...], weights, ((1,), (1,)))
    branch[...] = product.astype(bf16).astype(f32)
    rows = 4
    span = rows * STRIDE + 8
    for lane in range(0, width, LANES):
        lanes = slice(lane, lane + LANES)
        taps = [taps_ref[k : k + 1, lanes] for k in range(9)]
        for h in range(0, height, rows):
            windows = [
                branch[(h + i) * STRIDE : (h + i) * STRIDE + span, lanes] for i in range(3)
            ]
            left, middle, right = [
                windows[0] * taps[j] + windows[1] * taps[3 + j] + windows[2] * taps[6 + j]
                for j in range(3)
            ]
            convolved = (
                middle
                + pltpu.roll(left, 1, 0)
                + pltpu.roll(right, span - 1, 0)
                + bias_ref[:, lanes]
            )
            activated = convolved / (1.0 + jnp.exp(-convolved))
            kept = activated[: rows * STRIDE].reshape(rows, STRIDE, LANES)[:, 8:, :]
            act_ref[h * breadth : (h + rows) * breadth, lanes] = kept.reshape(
                rows * breadth, LANES
            ).astype(bf16)
    across = dot(order[...], act_ref[...]).astype(bf16)
    turned_ref[...] = across
    step = pl.program_id(0)
    turned[:, pl.ds(pl.multiple_of(step * width, width), width)] = across

    @pl.when(step == pl.num_programs(0) - 1)
    def _():
        column_states(turned, *column_refs, *outs, slot_refs)


def filtered(x, gain, own, other, taps, bias, tokens, dt_bias, rate, slots):
    expand = bias.shape[1]
    padded, channels = x.shape
    width = 1024
    states = tokens // BLOCK * STATE + 16
    one = lambda c: (0, 0)
    piece = pl.BlockSpec((width // 4, 2 * channels), lambda c: (c, 0))
    return pl.pallas_call(
        filter_kernel,
        grid=(expand // width,),
        in_specs=[
            pl.BlockSpec((padded, channels), lambda c: (0, 0)),
            pl.BlockSpec((1, channels), lambda c: (0, 0)),
            piece,
            piece,
            pl.BlockSpec((9, width), lambda c: (0, c)),
            pl.BlockSpec((1, width), lambda c: (0, c)),
            *piece_specs(own.shape[0], 13, 14),
            pl.BlockSpec(dt_bias.shape, one),
            pl.BlockSpec(rate.shape, one),
        ],
        out_specs=[pl.BlockSpec((tokens, width), lambda c: (0, c))] * 2
        + [pl.BlockSpec((tokens, LANES), one)] * 4
        + [pl.BlockSpec((states, expand), one)] * (slots - 1),
        out_shape=[jax.ShapeDtypeStruct((tokens, expand), bf16)] * 2
        + [jax.ShapeDtypeStruct((tokens, LANES), t) for t in (bf16, bf16, f32, bf16)]
        + [jax.ShapeDtypeStruct((states, expand), bf16)] * (slots - 1),
        scratch_shapes=[
            pltpu.VMEM((padded, channels), bf16),
            pltpu.VMEM((padded, width), f32),
            pltpu.VMEM((tokens, tokens), bf16),
            pltpu.VMEM((tokens, expand), bf16),
        ],
        compiler_params=pltpu.CompilerParams(vmem_limit_bytes=GRANT),
        cost_estimate=pl.CostEstimate(
            flops=2 * padded * channels * expand, bytes_accessed=6 * 2**20, transcendentals=tokens * expand
        ),
        name="norm_project_filter",
    )(x, gain, own, other, taps, bias, own, other, own, other, dt_bias, rate)


def mix_kernel(a_ref, coefs_ref, steps_ref, sums_ref, out_ref, spread, *scratch):
    @pl.when(pl.program_id(0) == 0)
    def _():
        for d, matrix in enumerate(head_spread(a_ref.shape[1])):
            spread[d] = matrix

    for c in range(a_ref.shape[0] // CHUNK):
        at = slice(c * CHUNK, (c + 1) * CHUNK)

        def store(span, lanes, value):
            out_ref[c * CHUNK + span.start : c * CHUNK + span.stop, lanes] = value

        mix_chunk(
            a_ref[at, :],
            coefs_ref[at, :],
            steps_ref[at, :].astype(f32),
            sums_ref[at, :],
            [spread[0], spread[1]],
            scratch,
            lambda lanes: None,
            store,
        )


def mixed_columns(values, coefs, steps, sums):
    tokens, expand = values.shape
    rows = 2 * CHUNK
    block = pl.BlockSpec((rows, expand), lambda i: (i, 0))
    thin = pl.BlockSpec((rows, LANES), lambda i: (i, 0))
    return pl.pallas_call(
        mix_kernel,
        grid=(tokens // rows,),
        in_specs=[block, thin, thin, thin],
        out_specs=block,
        out_shape=jax.ShapeDtypeStruct((tokens, expand), bf16),
        scratch_shapes=[pltpu.VMEM((2, LANES, expand), bf16), *mixing_scratch()],
        compiler_params=pltpu.CompilerParams(vmem_limit_bytes=GRANT),
        cost_estimate=pl.CostEstimate(
            flops=2**32, bytes_accessed=3 * 2**20, transcendentals=2**21
        ),
        name="mix_columns",
    )(values, coefs, steps, sums)


def entering_kernel(
    local_ref, read_ref, act_ref, skip_ref, x_ref, gain_ref, own_gate, other_gate, own_out, other_out, *refs
):
    place = here()
    slots = len(refs) - 5
    slot_refs, (part_ref, gate_ref, w_out_ref, w_gate, columns) = refs[:slots], refs[slots:]
    expand = local_ref.shape[1]
    states = slot_refs[0].shape[0] - 16
    groups = local_ref.shape[0] // CHUNK
    part = states // groups
    lines = part // STATE
    height = CHUNK // lines
    spread = head_spread(expand)
    row = place[0]
    decays = [ref[states:, :].astype(f32) for ref in slot_refs]
    for g in range(groups):
        at = slice(g * CHUNK, (g + 1) * CHUNK)
        total = local_ref[at, :].astype(f32)
        read = read_ref[at, :]
        for d in range(2):
            order = range(slots) if d == 0 else range(slots - 1, -1, -1)
            entering, product = [], [None] * lines
            sums = [jnp.zeros((STATE, expand), f32)] * lines
            for step, k in enumerate(order):
                reaches = row > step if d == 0 else row + step + 1 <= slots
                for line in range(lines):
                    at_state = g * part + line * STATE
                    state = slot_refs[k][at_state : at_state + STATE, :].astype(f32)
                    if product[line] is not None:
                        state = state * product[line]
                    sums[line] = sums[line] + jnp.where(reaches, state, 0.0)
                    fade = decays[k][g * lines + line : g * lines + line + 1, :]
                    product[line] = fade if product[line] is None else product[line] * fade
            entering = jnp.concatenate(sums, axis=0).astype(bf16)
            carried = dot(by_block(read, 64 * d + 48), entering)
            total = total + dot(read, spread[d]) * carried
        columns[at, :] = total.astype(bf16)
    w_gate[...] = input_weights(own_gate, other_gate, place[1] % 2)
    w_out_ref[...] = rows_of_eight(*paired(own_out, other_out, place[1] % 2))
    tokens = local_ref.shape[0]
    breadth = tokens // height
    for g in range(groups):
        at = slice(g * CHUNK, (g + 1) * CHUNK)
        to = lax.broadcasted_iota(jnp.int32, (CHUNK, tokens), 0) + g * CHUNK
        source = lax.broadcasted_iota(jnp.int32, (CHUNK, tokens), 1)
        w, h = source // height, source % height
        back = (to == h * breadth + w).astype(f32).astype(bf16)
        direct = skip_ref[...] * act_ref[at, :].astype(f32)
        part_ref[at, :] = dot(back, columns[...]) + direct
        normed = normalized(x_ref[at, :].astype(f32), gain_ref[...]).astype(bf16)
        gating = dot(normed, w_gate[...], ((1,), (1,))).astype(bf16).astype(f32)
        gate_ref[at, :] = (gating / (1.0 + jnp.exp(-gating))).astype(bf16)


def entered(local, read, act, skip, x, gain, own, other, slots):
    tokens, expand = local.shape
    pairs, channels = own.shape[0], x.shape[1]
    whole = lambda x: pl.BlockSpec(x.shape, lambda i: (0, 0))
    gate = pl.BlockSpec((pairs // 2, 2 * channels), lambda i: (1, 0))
    last = pl.BlockSpec((pairs, channels), lambda i: (0, 2))
    shapes = [
        jax.ShapeDtypeStruct((tokens, expand), f32),
        jax.ShapeDtypeStruct((tokens, expand), bf16),
        jax.ShapeDtypeStruct((expand, channels), bf16),
    ]
    return pl.pallas_call(
        entering_kernel,
        grid=(1,),
        in_specs=[whole(a) for a in (local, read, act, skip, x, gain)]
        + [gate, gate, last, last]
        + [whole(a) for a in slots],
        out_specs=[whole(a) for a in shapes],
        out_shape=shapes,
        scratch_shapes=[
            pltpu.VMEM((expand, channels), bf16),
            pltpu.VMEM((tokens, expand), bf16),
        ],
        compiler_params=pltpu.CompilerParams(vmem_limit_bytes=GRANT),
        cost_estimate=pl.CostEstimate(
            flops=2**32, bytes_accessed=12 * 2**20, transcendentals=2**19
        ),
        name="enter_columns",
    )(local, read, act, skip, x, gain, own, other, own, other, *slots)


def output_kernel(part_ref, gate_ref, rows_ref, x_ref, w_ref, out_gain_ref, out_ref):
    summed = part_ref[...] + rows_ref[...].astype(f32)
    mixed = (normalized(summed, out_gain_ref[...]) * gate_ref[...].astype(f32)).astype(bf16)
    out_ref[...] = (x_ref[...].astype(f32) + dot(mixed, w_ref[...])).astype(bf16)


def projected(part, gate, rows, x, w_out, out_gain):
    tokens, expand = part.shape
    channels = x.shape[1]
    block = 256
    one = lambda i: (0, 0)
    wide = pl.BlockSpec((block, expand), lambda i: (i, 0))
    narrow = pl.BlockSpec((block, channels), lambda i: (i, 0))
    return pl.pallas_call(
        output_kernel,
        grid=(tokens // block,),
        in_specs=[
            wide,
            wide,
            wide,
            narrow,
            pl.BlockSpec((expand, channels), one),
            pl.BlockSpec((1, expand), one),
        ],
        out_specs=narrow,
        out_shape=jax.ShapeDtypeStruct((tokens, channels), bf16),
        compiler_params=pltpu.CompilerParams(vmem_limit_bytes=GRANT),
        name="gate_and_project",
    )(part, gate, rows, x, w_out, out_gain)


def on_device(
    tokens, tile_mask, norm_gain, w_in, conv_weight, conv_bias, w_proj, dt_bias, decay_rate, skip_gain, out_gain, w_out
):
    wide = ("chip", "core")
    count_row, count_chip = lax.axis_size("row"), lax.axis_size("chip")
    height, breadth, channels = tokens.shape
    local = height * breadth
    expand = conv_bias.shape[0]

    groups = count_row * count_chip
    parcel = parcels(tile_mask.T, w_in.T, w_out, w_proj, groups)
    own = lax.all_to_all(parcel, ("row", "chip"), 0, 0, tiled=True)
    above, below = shifted(tokens[-1:], "row", 1), shifted(tokens[:1], "row", -1)
    tall = jnp.concatenate([above, tokens, below], axis=0)
    before, after = [
        jnp.concatenate(
            [
                diagonal(tokens[-1:, edge], 1, step),
                shifted(tokens[:, edge], wide, step),
                diagonal(tokens[:1, edge], -1, step),
            ],
            axis=0,
        )
        for edge, step in ((slice(breadth - 1, breadth), 1), (slice(0, 1), -1))
    ]
    after_last = jnp.concatenate([jnp.zeros_like(after[:1]), after], axis=0)
    body = jnp.concatenate(
        [after_last[:-1], jnp.zeros((height + 2, 6, channels), bf16), before, tall], axis=1
    ).reshape((height + 2) * STRIDE, channels)
    x_ext = jnp.concatenate([body, after_last[-1], jnp.zeros((15, channels), bf16)], axis=0)

    own, x_ext = lax.optimization_barrier((own, x_ext))
    other = lax.ppermute(own, "core", [(0, 1), (1, 0)])
    own, other = [p.reshape(groups * 8, p.shape[2]) for p in (own, other)]

    act, turned, coefs, steps, sums, read, *states = filtered(
        x_ext,
        norm_gain.reshape(1, -1),
        own,
        other,
        conv_weight,
        conv_bias.reshape(1, -1),
        local,
        dt_bias,
        decay_rate,
        count_row,
    )
    def spun(piece, d):
        return lax.ppermute(piece, "row", [(i, (i + d) % count_row) for i in range(count_row)])

    def dealt(x):
        return lax.all_to_all(
            x.reshape(-1, breadth, expand), wide, 0, 0, tiled=True
        ).reshape(-1, expand)

    lines = dealt(act)
    received = [spun(piece, d + 1) for d, piece in enumerate(states)]
    columns_local = mixed_columns(turned, coefs, steps, sums)
    lines, columns_local = lax.optimization_barrier((lines, columns_local))
    rows_out = swept_lines(lines, own, other, dt_bias, decay_rate)
    rows_out, received = lax.optimization_barrier((rows_out, received))
    rows_back = dealt(rows_out)
    x = tokens.reshape(local, channels)
    part, gate, full_out = entered(
        columns_local,
        read,
        act,
        skip_gain.reshape(1, -1),
        x,
        norm_gain.reshape(1, -1),
        own,
        other,
        received,
    )
    result = projected(part, gate, rows_back, x, full_out, out_gain.reshape(1, -1))
    return result.reshape(height, breadth, channels)


def solution(mesh):
    rows, columns = mesh.devices.shape
    split = Mesh(mesh.devices.reshape(rows, columns // 2, 2), ("row", "chip", "core"))
    wide, all_axes = ("chip", "core"), ("row", "chip", "core")
    placed = (
        P("row", wide, None),
        P("row", wide),
        P(),
        P(None, all_axes),
        P(),
        P(),
        P(all_axes, None),
        P(),
        P(),
        P(),
        P(),
        P(all_axes, None),
    )
    return jax.shard_map(
        on_device, mesh=split, in_specs=placed, out_specs=P("row", wide, None), check_vma=False
    )
```

```python
import jax
import jax.numpy as jnp
from jax import lax
from jax.experimental import pallas as pl
from jax.experimental.pallas import tpu as pltpu
from jax.sharding import Mesh, PartitionSpec as P

STATE = 16
HEADS = 32
TILE = 16
CHUNK = 128
LANES = 128
BLOCK = 32
PARTS = CHUNK // BLOCK
STRIDE = 24
LOG2E = 1.4426950408889634
GRANT = 56 * 2**20

f32 = jnp.float32
bf16 = jnp.bfloat16


def dot(a, b, contract=((1,), (0,))):
    return lax.dot_general(a, b, (contract, ((), ())), preferred_element_type=f32)


def shifted(x, axis, step):
    count = lax.axis_size(axis)
    pairs = [(i, i + step) for i in range(count) if 0 <= i + step < count]
    return lax.ppermute(x, axis, pairs)


def diagonal(x, down, right):
    axes = ("row", "chip", "core")
    rows, columns = lax.axis_size("row"), lax.axis_size(("chip", "core"))
    pairs = [
        (r * columns + c, (r + down) * columns + c + right)
        for r in range(rows)
        for c in range(columns)
        if 0 <= r + down < rows and 0 <= c + right < columns
    ]
    return lax.ppermute(x, axes, pairs)


def here():
    return lax.axis_index("row"), 2 * lax.axis_index("chip") + lax.axis_index("core")


def normalized(x, gain):
    average = jnp.mean(x, axis=-1, keepdims=True)
    centered = x - average
    spread = jnp.mean(centered * centered, axis=-1, keepdims=True)
    return centered * lax.rsqrt(spread + 1e-05) * gain


def paired(own_ref, other_ref, core):
    own, other = own_ref[...].astype(f32), other_ref[...].astype(f32)
    return jnp.where(core == 0, own, other), jnp.where(core == 0, other, own)


def rows_of_eight(*pieces):
    count = pieces[0].shape[0] // 8
    parts = [p.reshape(count, 8, p.shape[1]) for p in pieces]
    return jnp.concatenate(parts, axis=1).reshape(-1, pieces[0].shape[1]).astype(bf16)


def input_weights(own_ref, other_ref, core):
    half = own_ref.shape[1] // 2
    even, odd = paired(own_ref, other_ref, core)
    return rows_of_eight(even[:, :half], even[:, half:], odd[:, :half], odd[:, half:])


def parcel_kernel(mask, in_ref, out_ref, proj_ref, parcel_ref):
    place = here()
    row = lax.broadcasted_iota(jnp.int32, (8, LANES), 0)
    lane = lax.broadcasted_iota(jnp.int32, (8, LANES), 1)
    flags = jnp.zeros((8, LANES), f32)
    for i in range(mask.shape[1]):
        flags = jnp.where(
            (row == i) & (lane == place[1]), mask[:, i : i + 1].astype(f32), flags
        )
    turned = in_ref[...].astype(f32)
    parts = [turned[:8], turned[8:], out_ref[...].astype(f32), proj_ref[...].astype(f32), flags]
    at = 0
    for part in parts:
        width = part.shape[1]
        parcel_ref[:, :, at : at + width] = jnp.broadcast_to(
            part.astype(bf16)[None], (parcel_ref.shape[0], 8, width)
        )
        at += width


def parcels(mask, turned, w_out, w_proj, groups):
    width = 2 * turned.shape[1] + w_out.shape[1] + w_proj.shape[1] + LANES
    block = 32
    one = lambda i: (0, 0)
    return pl.pallas_call(
        parcel_kernel,
        grid=(groups // block,),
        in_specs=[
            pl.BlockSpec(mask.shape, one),
            pl.BlockSpec(turned.shape, one),
            pl.BlockSpec(w_out.shape, one),
            pl.BlockSpec(w_proj.shape, one),
        ],
        out_specs=pl.BlockSpec((block, 8, width), lambda i: (i, 0, 0)),
        out_shape=jax.ShapeDtypeStruct((groups, 8, width), bf16),
        compiler_params=pltpu.CompilerParams(vmem_limit_bytes=GRANT),
        name="parcels",
    )(mask, turned, w_out, w_proj)


def head_lanes(ref, first):
    heads = ref.shape[1]
    head = lax.broadcasted_iota(jnp.int32, (heads, LANES), 0)
    lane = lax.broadcasted_iota(jnp.int32, (heads, LANES), 1)
    placed = [
        lax.dot_general(
            ref[...],
            (lane == head + 64 * d).astype(f32),
            (((1,), (0,)), ((), ())),
            precision=lax.Precision.HIGHEST,
            preferred_element_type=f32,
        )
        for d in range(2)
    ]
    return placed[0][first : first + 1] + placed[1][first + 1 : first + 2]


def chunk_terms(values, w_proj, bias, rate, kept):
    coefs = dot(values, w_proj)
    at = lax.broadcasted_iota(jnp.int32, (CHUNK, LANES), 0)
    lane = lax.broadcasted_iota(jnp.int32, (CHUNK, LANES), 1)
    v = coefs + bias
    steps = kept * (jnp.maximum(v, 0.0) + jnp.log1p(jnp.exp(-jnp.abs(v))))
    decays = steps * rate
    lower = ((lane <= at) & (lane // BLOCK == at // BLOCK)).astype(f32).astype(bf16)
    high = decays.astype(bf16)
    rest = decays - high.astype(f32)
    middle = rest.astype(bf16)
    low = (rest - middle.astype(f32)).astype(bf16)
    total = dot(
        jnp.concatenate([lower] * 3, axis=1), jnp.concatenate([high, middle, low], axis=0)
    )
    sums = jnp.where(lane < 64, total, total - decays)
    ends = [total[(b + 1) * BLOCK - 1 : (b + 1) * BLOCK, :] for b in range(PARTS)]
    return coefs, steps, sums, ends


def edge_factors(sums, steps, ends):
    lane = lax.broadcasted_iota(jnp.int32, (CHUNK, LANES), 1)
    end = jnp.concatenate([jnp.broadcast_to(e, (BLOCK, LANES)) for e in ends], axis=0)
    tail = jnp.exp2(jnp.where(lane < 64, sums - end, -sums)) * steps
    enter = jnp.exp2(jnp.where(lane < 64, -sums, sums - end))
    rows = ends + [jnp.zeros((8 - PARTS, LANES), f32)]
    fade = jnp.exp2(-jnp.concatenate(rows, axis=0))
    return tail.astype(bf16), enter.astype(bf16), fade


def head_spread(expand):
    head = lax.broadcasted_iota(jnp.int32, (LANES, expand), 0)
    channel = lax.broadcasted_iota(jnp.int32, (LANES, expand), 1)
    return [(head == channel // 32 + 64 * d).astype(f32).astype(bf16) for d in range(2)]


def by_block(coefs, first):
    lane = lax.broadcasted_iota(jnp.int32, (LANES, PARTS * STATE), 0)
    to = lax.broadcasted_iota(jnp.int32, (LANES, PARTS * STATE), 1)
    copied = dot(coefs, (lane == first + to % STATE).astype(f32).astype(bf16))
    at = lax.broadcasted_iota(jnp.int32, copied.shape, 0)
    place = lax.broadcasted_iota(jnp.int32, copied.shape, 1)
    return jnp.where(at // BLOCK == place // STATE, copied, 0.0).astype(bf16)


def block_states(values, coefs, tail, spread):
    writes, inputs = coefs.astype(bf16), values.astype(f32)
    states = []
    for d in range(2):
        weighted = (inputs * dot(tail, spread[d])).astype(bf16)
        states.append(dot(by_block(writes, 64 * d + 32), weighted, ((0,), (0,))))
    return states


def mixing_scratch():
    return [
        pltpu.VMEM((LANES, CHUNK), f32),
        pltpu.VMEM((LANES, CHUNK), f32),
        pltpu.VMEM((4 * PARTS, 8, LANES), f32),
    ]


def mix_chunk(values, coefs, steps, sums, spread, scratch, more, store):
    sums_t, steps_t, rows = scratch
    expand = values.shape[1]
    sums_t[...], steps_t[...] = sums.T, steps.T
    row_lane = lax.broadcasted_iota(jnp.int32, (8, LANES), 1)
    for a, (ref, first) in enumerate(((sums_t, 0), (sums_t, 64), (steps_t, 0), (steps_t, 64))):
        lines = [ref[pl.ds(first + k, 8, stride=4), :] for k in range(4)]
        for b in range(PARTS):
            merged = None
            for k in range(4):
                turn = (k - b) * BLOCK % LANES
                line = pltpu.roll(lines[k], turn, 1) if turn else lines[k]
                merged = line if merged is None else jnp.where(row_lane // BLOCK == k, line, merged)
            rows[a * PARTS + b] = merged
    at = lax.broadcasted_iota(jnp.int32, (BLOCK, LANES), 0)
    source = lax.broadcasted_iota(jnp.int32, (BLOCK, LANES), 1) % BLOCK
    causal = source <= at
    c = coefs.astype(bf16)
    products = []
    for b in range(PARTS):
        block = c[b * BLOCK : (b + 1) * BLOCK, :]
        four = jnp.concatenate([block] * 4, axis=0)
        forward = dot(block[:, 48:64], four[:, 32:48], ((1,), (1,)))
        backward = dot(block[:, 112:128], four[:, 96:112], ((1,), (1,)))
        products.append(
            (jnp.where(causal, forward, 0.0), jnp.where(source >= at, backward, 0.0))
        )
    high = sums.astype(bf16)
    parts = jnp.concatenate([high, (sums - high.astype(f32)).astype(bf16)], axis=1)
    head_of = lax.broadcasted_iota(jnp.int32, (BLOCK, LANES), 1) // 32
    for pair in range(0, expand, 2 * LANES):
        wide = slice(pair, pair + 2 * LANES)
        own = [
            dot(parts, jnp.concatenate([spread[d][:, wide]] * 2, axis=0)) for d in range(2)
        ]
        extra = more(wide)
        for lane in range(0, 2 * LANES, LANES):
            tile = (pair + lane) // LANES
            lanes = slice(pair + lane, pair + lane + LANES)
            for b in range(PARTS):
                span = slice(b * BLOCK, (b + 1) * BLOCK)
                row = [rows[a * PARTS + b, tile : tile + 1, :] for a in range(4)]
                exponent = jnp.where(
                    causal,
                    row[0] - own[0][span, lane : lane + LANES],
                    own[1][span, lane : lane + LANES] - row[1],
                )
                scale = products[b][0] * row[2] + products[b][1] * row[3]
                mixing = (jnp.exp2(exponent) * scale).astype(bf16)
                inputs = values[span, lanes]
                apart = jnp.concatenate(
                    [jnp.where(head_of == k, inputs, jnp.zeros_like(inputs)) for k in range(4)],
                    axis=0,
                )
                total = dot(mixing, apart)
                if extra is not None:
                    total = total + extra[span, lane : lane + LANES]
                store(span, lanes, total.astype(bf16))


def line_kernel(
    a_ref, own_ref, other_ref, own_flags, other_flags, bias_ref, rate_ref, out_ref, coefs, steps, sums, enters, fades, states, entering, *scratch
):
    place = here()
    length, expand = a_ref.shape
    chunks = length // CHUNK
    part = PARTS * STATE
    lane = lax.broadcasted_iota(jnp.int32, (CHUNK, LANES), 1)
    spread = head_spread(expand)
    w_proj = rows_of_eight(*paired(own_ref, other_ref, place[1] % 2))
    bias, rate = head_lanes(bias_ref, 0), head_lanes(rate_ref, 0) * LOG2E
    flags = own_flags[...].astype(f32) + other_flags[...].astype(f32)
    line = lax.broadcasted_iota(jnp.int32, flags.shape, 0)
    mine = (line // (flags.shape[0] // 4) == place[0]) & (line % 8 == place[1] // TILE)
    mask = jnp.sum(jnp.where(mine, flags, 0.0), axis=0, keepdims=True)
    position = lax.broadcasted_iota(jnp.int32, (CHUNK, LANES), 0)
    for c in range(chunks):
        tile_at = lane == (position + c * CHUNK) // TILE
        kept = jnp.sum(jnp.where(tile_at, mask, 0.0), axis=1, keepdims=True)
        at = slice(c * CHUNK, (c + 1) * CHUNK)
        values = a_ref[at, :]
        k, s, q, ends = chunk_terms(values, w_proj, bias, rate, kept)
        tail, enter, fade = edge_factors(q, s, ends)
        coefs[at, :], steps[at, :], sums[at, :], enters[at, :] = k, s, q, enter
        fades[8 * c : 8 * c + 8, :] = fade
        for d, state in enumerate(block_states(values, k, tail, spread)):
            states[d, c * part : (c + 1) * part, :] = state
    fade = fades[...]
    high = fade.astype(bf16)
    low = (fade - high.astype(f32)).astype(bf16)
    blocks = chunks * PARTS
    for d in range(2):
        decay = dot(high, spread[d]) + dot(low, spread[d])
        running = jnp.zeros((STATE, expand), f32)
        for b in range(blocks) if d == 0 else range(blocks - 1, -1, -1):
            at = slice(b * STATE, (b + 1) * STATE)
            entering[d, at, :] = running.astype(bf16)
            row = b // PARTS * 8 + b % PARTS
            running = running * decay[row : row + 1, :] + states[d, at, :]
    for c in range(chunks):
        at = slice(c * CHUNK, (c + 1) * CHUNK)
        k, enter = coefs[at, :], enters[at, :]
        read = k.astype(bf16)
        reads = [by_block(read, 64 * d + 48) for d in range(2)]

        def carried(lanes):
            total = None
            for d in range(2):
                state = dot(reads[d], entering[d, c * part : (c + 1) * part, lanes])
                term = dot(enter, spread[d][:, lanes]) * state
                total = term if total is None else total + term
            return total

        def store(span, lanes, value):
            out_ref[c * CHUNK + span.start : c * CHUNK + span.stop, lanes] = value

        mix_chunk(
            a_ref[at, :], k, steps[at, :], sums[at, :], spread, scratch, carried, store
        )


def piece_specs(rows, *columns):
    return [pl.BlockSpec((rows, LANES), lambda i, c=c: (0, c)) for c in columns for _ in range(2)]


def swept_lines(values, own, other, bias, rate):
    length, expand = values.shape
    chunks = length // CHUNK
    small = pl.BlockSpec(bias.shape, lambda i: (0, 0))
    return pl.pallas_call(
        line_kernel,
        grid=(1,),
        in_specs=[
            pl.BlockSpec((length, expand), lambda i: (0, 0)),
            *piece_specs(own.shape[0], 12, 14),
            small,
            small,
        ],
        out_specs=pl.BlockSpec((length, expand), lambda i: (0, 0)),
        out_shape=jax.ShapeDtypeStruct((length, expand), bf16),
        scratch_shapes=[
            pltpu.VMEM((length, LANES), f32),
            pltpu.VMEM((length, LANES), f32),
            pltpu.VMEM((length, LANES), f32),
            pltpu.VMEM((length, LANES), bf16),
            pltpu.VMEM((8 * chunks, LANES), f32),
            pltpu.VMEM((2, length // BLOCK * STATE, expand), f32),
            pltpu.VMEM((2, length // BLOCK * STATE, expand), bf16),
            *mixing_scratch(),
        ],
        compiler_params=pltpu.CompilerParams(vmem_limit_bytes=30 * 2**20),
        cost_estimate=pl.CostEstimate(
            flops=6 * 2**30, bytes_accessed=3 * 2**20, transcendentals=2**21
        ),
        name="sweep_rows",
    )(values, own, other, own, other, bias, rate)


def column_states(
    values_ref, own_ref, other_ref, own_flags, other_flags, bias_ref, rate_ref, coefs_ref, steps_ref, sums_ref, read_ref, slot_refs
):
    row, column = here()
    expand = values_ref.shape[1]
    slots = len(slot_refs)
    states = slot_refs[0].shape[0] - 16
    groups = values_ref.shape[0] // CHUNK
    part = states // groups
    lane = lax.broadcasted_iota(jnp.int32, (CHUNK, LANES), 1)
    flags = (own_flags[...].astype(f32) + other_flags[...].astype(f32)).astype(bf16)
    to = lax.broadcasted_iota(jnp.int32, (CHUNK, flags.shape[0]), 0)
    source = lax.broadcasted_iota(jnp.int32, (CHUNK, flags.shape[0]), 1)
    mine = (source // (flags.shape[0] // (slots + 1)) == row) & (
        source % 8 == to % BLOCK // TILE
    )
    marks = dot(mine.astype(f32).astype(bf16), flags)
    kept = jnp.sum(jnp.where(lane == column, marks, 0.0), axis=1, keepdims=True)
    proj = rows_of_eight(*paired(own_ref, other_ref, column % 2))
    bias, rate = head_lanes(bias_ref, 2), head_lanes(rate_ref, 2) * LOG2E
    spread = head_spread(expand)
    rows = [[] for _ in slot_refs]
    for g in range(groups):
        at = slice(g * CHUNK, (g + 1) * CHUNK)
        values = values_ref[at, :]
        k, s, q, ends = chunk_terms(values, proj, bias, rate, kept)
        coefs_ref[at, :], steps_ref[at, :], sums_ref[at, :] = k.astype(bf16), s.astype(bf16), q
        tail, enter, fade = edge_factors(q, s, ends)
        read_ref[at, :] = jnp.where(lane % 64 >= 48, k.astype(bf16), enter)
        high = fade.astype(bf16)
        low = (fade - high.astype(f32)).astype(bf16)
        down, up = block_states(values, k, tail, spread)
        fades = [dot(high, m) + dot(low, m) for m in spread]
        for d, ref in enumerate(slot_refs):
            onward = row + d + 1 <= slots
            ref[g * part : (g + 1) * part, :] = jnp.where(onward, down, up).astype(bf16)
            rows[d].append(jnp.where(onward, fades[0], fades[1])[:PARTS])
    for d, ref in enumerate(slot_refs):
        ref[states:, :] = jnp.concatenate(rows[d], axis=0).astype(bf16)


def filter_kernel(
    x_ref, gain_ref, own_ref, other_ref, taps_ref, bias_ref, *refs
):
    place = here()
    column_refs, (act_ref, turned_ref), refs = refs[:6], refs[6:8], refs[8:]
    outs, slot_refs, (normed, branch, order, turned) = refs[:4], refs[4:-4], refs[-4:]
    padded = x_ref.shape[0]
    tokens, width = act_ref.shape
    height = padded // STRIDE - 2
    breadth = tokens // height

    @pl.when(pl.program_id(0) == 0)
    def _():
        step = 64
        for at in range(0, padded, step):
            x = x_ref[at : at + step, :].astype(f32)
            normed[at : at + step, :] = normalized(x, gain_ref[...]).astype(bf16)
        to = lax.broadcasted_iota(jnp.int32, (tokens, tokens), 0)
        source = lax.broadcasted_iota(jnp.int32, (tokens, tokens), 1)
        w, h = to // height, to % height
        order[...] = (source == h * breadth + w).astype(f32).astype(bf16)

    weights = input_weights(own_ref, other_ref, place[1] % 2)
    product = dot(normed[...], weights, ((1,), (1,)))
    branch[...] = product.astype(bf16).astype(f32)
    rows = 4
    span = rows * STRIDE + 8
    for lane in range(0, width, LANES):
        lanes = slice(lane, lane + LANES)
        taps = [taps_ref[k : k + 1, lanes] for k in range(9)]
        for h in range(0, height, rows):
            windows = [
                branch[(h + i) * STRIDE : (h + i) * STRIDE + span, lanes] for i in range(3)
            ]
            left, middle, right = [
                windows[0] * taps[j] + windows[1] * taps[3 + j] + windows[2] * taps[6 + j]
                for j in range(3)
            ]
            convolved = (
                middle
                + pltpu.roll(left, 1, 0)
                + pltpu.roll(right, span - 1, 0)
                + bias_ref[:, lanes]
            )
            half = 0.5 * convolved
            activated = half + half * jnp.tanh(half)
            kept = activated[: rows * STRIDE].reshape(rows, STRIDE, LANES)[:, 8:, :]
            act_ref[h * breadth : (h + rows) * breadth, lanes] = kept.reshape(
                rows * breadth, LANES
            ).astype(bf16)
    across = dot(order[...], act_ref[...]).astype(bf16)
    turned_ref[...] = across
    step = pl.program_id(0)
    turned[:, pl.ds(pl.multiple_of(step * width, width), width)] = across

    @pl.when(step == pl.num_programs(0) - 1)
    def _():
        column_states(turned, *column_refs, *outs, slot_refs)


def filtered(x, gain, own, other, taps, bias, tokens, dt_bias, rate, slots):
    expand = bias.shape[1]
    padded, channels = x.shape
    width = 1024
    states = tokens // BLOCK * STATE + 16
    one = lambda c: (0, 0)
    piece = pl.BlockSpec((width // 4, 2 * channels), lambda c: (c, 0))
    return pl.pallas_call(
        filter_kernel,
        grid=(expand // width,),
        in_specs=[
            pl.BlockSpec((padded, channels), lambda c: (0, 0)),
            pl.BlockSpec((1, channels), lambda c: (0, 0)),
            piece,
            piece,
            pl.BlockSpec((9, width), lambda c: (0, c)),
            pl.BlockSpec((1, width), lambda c: (0, c)),
            *piece_specs(own.shape[0], 13, 14),
            pl.BlockSpec(dt_bias.shape, one),
            pl.BlockSpec(rate.shape, one),
        ],
        out_specs=[pl.BlockSpec((tokens, width), lambda c: (0, c))] * 2
        + [pl.BlockSpec((tokens, LANES), one)] * 4
        + [pl.BlockSpec((states, expand), one)] * (slots - 1),
        out_shape=[jax.ShapeDtypeStruct((tokens, expand), bf16)] * 2
        + [jax.ShapeDtypeStruct((tokens, LANES), t) for t in (bf16, bf16, f32, bf16)]
        + [jax.ShapeDtypeStruct((states, expand), bf16)] * (slots - 1),
        scratch_shapes=[
            pltpu.VMEM((padded, channels), bf16),
            pltpu.VMEM((padded, width), f32),
            pltpu.VMEM((tokens, tokens), bf16),
            pltpu.VMEM((tokens, expand), bf16),
        ],
        compiler_params=pltpu.CompilerParams(vmem_limit_bytes=GRANT),
        cost_estimate=pl.CostEstimate(
            flops=2 * padded * channels * expand, bytes_accessed=6 * 2**20, transcendentals=tokens * expand
        ),
        name="norm_project_filter",
    )(x, gain, own, other, taps, bias, own, other, own, other, dt_bias, rate)


def mix_kernel(a_ref, coefs_ref, steps_ref, sums_ref, out_ref, spread, *scratch):
    @pl.when(pl.program_id(0) == 0)
    def _():
        for d, matrix in enumerate(head_spread(a_ref.shape[1])):
            spread[d] = matrix

    for c in range(a_ref.shape[0] // CHUNK):
        at = slice(c * CHUNK, (c + 1) * CHUNK)

        def store(span, lanes, value):
            out_ref[c * CHUNK + span.start : c * CHUNK + span.stop, lanes] = value

        mix_chunk(
            a_ref[at, :],
            coefs_ref[at, :],
            steps_ref[at, :].astype(f32),
            sums_ref[at, :],
            [spread[0], spread[1]],
            scratch,
            lambda lanes: None,
            store,
        )


def mixed_columns(values, coefs, steps, sums):
    tokens, expand = values.shape
    rows = 2 * CHUNK
    block = pl.BlockSpec((rows, expand), lambda i: (i, 0))
    thin = pl.BlockSpec((rows, LANES), lambda i: (i, 0))
    return pl.pallas_call(
        mix_kernel,
        grid=(tokens // rows,),
        in_specs=[block, thin, thin, thin],
        out_specs=block,
        out_shape=jax.ShapeDtypeStruct((tokens, expand), bf16),
        scratch_shapes=[pltpu.VMEM((2, LANES, expand), bf16), *mixing_scratch()],
        compiler_params=pltpu.CompilerParams(vmem_limit_bytes=GRANT),
        cost_estimate=pl.CostEstimate(
            flops=2**32, bytes_accessed=3 * 2**20, transcendentals=2**21
        ),
        name="mix_columns",
    )(values, coefs, steps, sums)


def entering_kernel(
    local_ref, read_ref, act_ref, skip_ref, x_ref, gain_ref, own_gate, other_gate, own_out, other_out, *refs
):
    place = here()
    slots = len(refs) - 5
    slot_refs, (part_ref, gate_ref, w_out_ref, w_gate, columns) = refs[:slots], refs[slots:]
    expand = local_ref.shape[1]
    states = slot_refs[0].shape[0] - 16
    groups = local_ref.shape[0] // CHUNK
    part = states // groups
    lines = part // STATE
    height = CHUNK // lines
    spread = head_spread(expand)
    row = place[0]
    decays = [ref[states:, :].astype(f32) for ref in slot_refs]
    for g in range(groups):
        at = slice(g * CHUNK, (g + 1) * CHUNK)
        total = local_ref[at, :].astype(f32)
        read = read_ref[at, :]
        for d in range(2):
            order = range(slots) if d == 0 else range(slots - 1, -1, -1)
            entering, product = [], [None] * lines
            sums = [jnp.zeros((STATE, expand), f32)] * lines
            for step, k in enumerate(order):
                reaches = row > step if d == 0 else row + step + 1 <= slots
                for line in range(lines):
                    at_state = g * part + line * STATE
                    state = slot_refs[k][at_state : at_state + STATE, :].astype(f32)
                    if product[line] is not None:
                        state = state * product[line]
                    sums[line] = sums[line] + jnp.where(reaches, state, 0.0)
                    fade = decays[k][g * lines + line : g * lines + line + 1, :]
                    product[line] = fade if product[line] is None else product[line] * fade
            entering = jnp.concatenate(sums, axis=0).astype(bf16)
            carried = dot(by_block(read, 64 * d + 48), entering)
            total = total + dot(read, spread[d]) * carried
        columns[at, :] = total.astype(bf16)
    w_gate[...] = input_weights(own_gate, other_gate, place[1] % 2)
    w_out_ref[...] = rows_of_eight(*paired(own_out, other_out, place[1] % 2))
    tokens = local_ref.shape[0]
    breadth = tokens // height
    for g in range(groups):
        at = slice(g * CHUNK, (g + 1) * CHUNK)
        to = lax.broadcasted_iota(jnp.int32, (CHUNK, tokens), 0) + g * CHUNK
        source = lax.broadcasted_iota(jnp.int32, (CHUNK, tokens), 1)
        w, h = source // height, source % height
        back = (to == h * breadth + w).astype(f32).astype(bf16)
        direct = skip_ref[...] * act_ref[at, :].astype(f32)
        part_ref[at, :] = dot(back, columns[...]) + direct
        normed = normalized(x_ref[at, :].astype(f32), gain_ref[...]).astype(bf16)
        gating = dot(normed, w_gate[...], ((1,), (1,))).astype(bf16).astype(f32)
        gate_ref[at, :] = (gating / (1.0 + jnp.exp(-gating))).astype(bf16)


def entered(local, read, act, skip, x, gain, own, other, slots):
    tokens, expand = local.shape
    pairs, channels = own.shape[0], x.shape[1]
    whole = lambda x: pl.BlockSpec(x.shape, lambda i: (0, 0))
    gate = pl.BlockSpec((pairs // 2, 2 * channels), lambda i: (1, 0))
    last = pl.BlockSpec((pairs, channels), lambda i: (0, 2))
    shapes = [
        jax.ShapeDtypeStruct((tokens, expand), f32),
        jax.ShapeDtypeStruct((tokens, expand), bf16),
        jax.ShapeDtypeStruct((expand, channels), bf16),
    ]
    return pl.pallas_call(
        entering_kernel,
        grid=(1,),
        in_specs=[whole(a) for a in (local, read, act, skip, x, gain)]
        + [gate, gate, last, last]
        + [whole(a) for a in slots],
        out_specs=[whole(a) for a in shapes],
        out_shape=shapes,
        scratch_shapes=[
            pltpu.VMEM((expand, channels), bf16),
            pltpu.VMEM((tokens, expand), bf16),
        ],
        compiler_params=pltpu.CompilerParams(vmem_limit_bytes=GRANT),
        cost_estimate=pl.CostEstimate(
            flops=2**32, bytes_accessed=12 * 2**20, transcendentals=2**19
        ),
        name="enter_columns",
    )(local, read, act, skip, x, gain, own, other, own, other, *slots)


def output_kernel(part_ref, gate_ref, rows_ref, x_ref, w_ref, out_gain_ref, out_ref):
    summed = part_ref[...] + rows_ref[...].astype(f32)
    mixed = (normalized(summed, out_gain_ref[...]) * gate_ref[...].astype(f32)).astype(bf16)
    out_ref[...] = (x_ref[...].astype(f32) + dot(mixed, w_ref[...])).astype(bf16)


def projected(part, gate, rows, x, w_out, out_gain):
    tokens, expand = part.shape
    channels = x.shape[1]
    block = 256
    one = lambda i: (0, 0)
    wide = pl.BlockSpec((block, expand), lambda i: (i, 0))
    narrow = pl.BlockSpec((block, channels), lambda i: (i, 0))
    return pl.pallas_call(
        output_kernel,
        grid=(tokens // block,),
        in_specs=[
            wide,
            wide,
            wide,
            narrow,
            pl.BlockSpec((expand, channels), one),
            pl.BlockSpec((1, expand), one),
        ],
        out_specs=narrow,
        out_shape=jax.ShapeDtypeStruct((tokens, channels), bf16),
        compiler_params=pltpu.CompilerParams(vmem_limit_bytes=GRANT),
        name="gate_and_project",
    )(part, gate, rows, x, w_out, out_gain)


def on_device(
    tokens, tile_mask, norm_gain, w_in, conv_weight, conv_bias, w_proj, dt_bias, decay_rate, skip_gain, out_gain, w_out
):
    wide = ("chip", "core")
    count_row, count_chip = lax.axis_size("row"), lax.axis_size("chip")
    height, breadth, channels = tokens.shape
    local = height * breadth
    expand = conv_bias.shape[0]

    groups = count_row * count_chip
    parcel = parcels(tile_mask.T, w_in.T, w_out, w_proj, groups)
    own = lax.all_to_all(parcel, ("row", "chip"), 0, 0, tiled=True)
    above, below = shifted(tokens[-1:], "row", 1), shifted(tokens[:1], "row", -1)
    tall = jnp.concatenate([above, tokens, below], axis=0)
    before, after = [
        jnp.concatenate(
            [
                diagonal(tokens[-1:, edge], 1, step),
                shifted(tokens[:, edge], wide, step),
                diagonal(tokens[:1, edge], -1, step),
            ],
            axis=0,
        )
        for edge, step in ((slice(breadth - 1, breadth), 1), (slice(0, 1), -1))
    ]
    after_last = jnp.concatenate([jnp.zeros_like(after[:1]), after], axis=0)
    body = jnp.concatenate(
        [after_last[:-1], jnp.zeros((height + 2, 6, channels), bf16), before, tall], axis=1
    ).reshape((height + 2) * STRIDE, channels)
    x_ext = jnp.concatenate([body, after_last[-1], jnp.zeros((15, channels), bf16)], axis=0)

    own, x_ext = lax.optimization_barrier((own, x_ext))
    other = lax.ppermute(own, "core", [(0, 1), (1, 0)])
    own, other = [p.reshape(groups * 8, p.shape[2]) for p in (own, other)]

    act, turned, coefs, steps, sums, read, *states = filtered(
        x_ext,
        norm_gain.reshape(1, -1),
        own,
        other,
        conv_weight,
        conv_bias.reshape(1, -1),
        local,
        dt_bias,
        decay_rate,
        count_row,
    )
    def spun(piece, d):
        return lax.ppermute(piece, "row", [(i, (i + d) % count_row) for i in range(count_row)])

    def dealt(x):
        return lax.all_to_all(
            x.reshape(-1, breadth, expand), wide, 0, 0, tiled=True
        ).reshape(-1, expand)

    lines = dealt(act)
    received = [spun(piece, d + 1) for d, piece in enumerate(states)]
    columns_local = mixed_columns(turned, coefs, steps, sums)
    lines, columns_local = lax.optimization_barrier((lines, columns_local))
    rows_out = swept_lines(lines, own, other, dt_bias, decay_rate)
    rows_out, received = lax.optimization_barrier((rows_out, received))
    rows_back = dealt(rows_out)
    x = tokens.reshape(local, channels)
    part, gate, full_out = entered(
        columns_local,
        read,
        act,
        skip_gain.reshape(1, -1),
        x,
        norm_gain.reshape(1, -1),
        own,
        other,
        received,
    )
    result = projected(part, gate, rows_back, x, full_out, out_gain.reshape(1, -1))
    return result.reshape(height, breadth, channels)


def solution(mesh):
    rows, columns = mesh.devices.shape
    split = Mesh(mesh.devices.reshape(rows, columns // 2, 2), ("row", "chip", "core"))
    wide, all_axes = ("chip", "core"), ("row", "chip", "core")
    placed = (
        P("row", wide, None),
        P("row", wide),
        P(),
        P(None, all_axes),
        P(),
        P(),
        P(all_axes, None),
        P(),
        P(),
        P(),
        P(),
        P(all_axes, None),
    )
    return jax.shard_map(
        on_device, mesh=split, in_specs=placed, out_specs=P("row", wide, None), check_vma=False
    )
```
